32 devices in a mesh: tm: 2 (over y), rows: 16 (over z, x, core).
Axes of the slice: x: 2, y: 2, z: 4, core: 2. Of those that a mesh axis runs over, the one named last changes fastest.
Arguments:
- inputs: bfloat16 [4, 64, 16, 256], P('tm', 'rows'), may hold values from -6 to 6
- cotangent: bfloat16 [4, 64, 16, 256], P('tm', 'rows'), may hold values from -6 to 6
- kernel: bfloat16 [27, 256, 256], P(None, 'rows', 'tm'), may hold values from -0.078125 to 0.078125
Outputs:
- grad_inputs: bfloat16 [4, 64, 16, 256], P('tm', 'rows')
- grad_kernel: float32 [27, 256, 256], P(None, 'rows', 'tm')
The draws below stay inside these ranges and needn't reach their ends.
All inputs are finite; a program needn't handle non-finite values.
Results may differ from the reference program's by a relative error of at most 0.003.
Values may be sent and summed in bfloat16 or wider, within the bound.
A program may use at most 64 MiB of HBM per device.

```python
import jax
import jax.numpy as jnp
from jax import lax

C = 256
WIDTH = 16
FRAMES = 4
HEIGHT = 64


def raised(array, rng, source, target, shards_of, factor):
    owner, partner = [(jnp.arange(array.shape[dim]) // (array.shape[dim] // shards_of)).reshape([-1 if axis == dim else 1 for axis in range(array.ndim)]) for dim in (source, target)]
    chosen = jax.random.permutation(rng, shards_of)[partner]
    strong = (owner == chosen) | (owner == (partner + shards_of // 2) % shards_of)
    return jnp.where(strong, factor * array, array)


def block_scale(rng, dims, split, smallest, top_value):
    level, own = 1.0, jax.random.fold_in(rng, 6)
    for axis_at, parts in split:
        draws = jnp.exp(jax.random.uniform(jax.random.fold_in(own, axis_at), (parts,), jnp.float32, smallest / len(split), top_value / len(split)))
        level = level * jnp.repeat(draws, dims[axis_at] // parts).reshape([-1 if axis == axis_at else 1 for axis in range(len(dims))])
    return level


def bell_draw(stream_key, extent, scale, reach, cuts=(), kind=jnp.bfloat16):
    result = scale * jax.random.normal(stream_key, extent, jnp.float32)
    if cuts:
        result = result * block_scale(stream_key, extent, cuts, -0.22, 0.18)
    return jnp.clip(result, -reach, reach).astype(kind)


def bell_draw_with(stream_key, extent, deviation, limit, shards, heavy, dtype=jnp.bfloat16):
    entries = deviation * jax.random.normal(stream_key, extent, jnp.float32)
    if shards:
        entries = entries * block_scale(stream_key, extent, shards, -0.22, 0.18)
    return jnp.clip(raised(entries, jax.random.fold_in(stream_key, 3), *heavy), -limit, limit).astype(dtype)


def setup_inputs(seed: int = 0) -> dict:
    key_of = jax.random.split(jax.random.key(seed), 4)
    inputs = bell_draw(key_of[0], (FRAMES, HEIGHT, WIDTH, C), 1.0, 6.0, ((0, 2), (1, 16)))
    cotangent = bell_draw_with(key_of[1], (FRAMES, HEIGHT, WIDTH, C), 1.0, 6.0, ((0, 2), (1, 16)), (1, 3, 16, 2.0))
    kernel = bell_draw(key_of[2], (27, C, C), (27 * C) ** -0.5, 0.078125, ((1, 16), (2, 2)))
    return {"inputs": inputs, "cotangent": cotangent, "kernel": kernel}


def silu_slope(values):
    logistic = jax.nn.sigmoid(values)
    return logistic * (1.0 + values * (1.0 - logistic))

def convolve_back(gradient, kernel):
    frames, height, across, channels = gradient.shape
    padded = jnp.pad(gradient, ((0, 2), (1, 1), (1, 1), (0, 0)))
    summed = jnp.zeros((frames * height * across, kernel.shape[1]), jnp.float32)
    for time_tap in range(3):
        for row_tap in range(3):
            for col_tap in range(3):
                window = padded[2 - time_tap:2 - time_tap + frames, 2 - row_tap:2 - row_tap + height, 2 - col_tap:2 - col_tap + across].reshape(-1, channels)
                summed = summed + jnp.dot(window, kernel[9 * time_tap + 3 * row_tap + col_tap].T, preferred_element_type=jnp.float32)
    return summed.reshape(frames, height, across, -1)

def kernel_grad(source, gradient):
    frames, height, across, channels = source.shape
    padded = jnp.pad(source, ((2, 0), (1, 1), (1, 1), (0, 0)))
    flat_grad = gradient.reshape(-1, gradient.shape[3])
    pieces = []
    for time_tap in range(3):
        for row_tap in range(3):
            for col_tap in range(3):
                window = padded[time_tap:time_tap + frames, row_tap:row_tap + height, col_tap:col_tap + across].reshape(-1, channels)
                pieces.append(lax.dot_general(window, flat_grad, (((0,), (0,)), ((), ())), preferred_element_type=jnp.float32))
    return jnp.stack(pieces, 0)

def reference(inputs, cotangent, kernel):
    frames, height, across, channels = inputs.shape
    act = jax.nn.silu(inputs.astype(jnp.float32)).astype(jnp.bfloat16)
    grad_act = convolve_back(cotangent, kernel)
    grad_inputs = (cotangent.astype(jnp.float32) + grad_act * silu_slope(inputs.astype(jnp.float32))).astype(jnp.bfloat16)
    factor = float(frames * height * across) ** (-0.5)
    grad_kernel = kernel_grad(act, cotangent) * factor
    return (grad_inputs, grad_kernel)
```

```python
import functools

import jax
import jax.numpy as jnp
from jax import lax
from jax.experimental import pallas as pl
from jax.experimental.pallas import tpu as pltpu
from jax.sharding import PartitionSpec as P

MESH = pl.DeviceIdType.MESH
LANES = 128


def extended(block, sides, width):
    for axis, dim in sides:
        count = lax.axis_size(axis)
        forward = [(i, i + 1) for i in range(count - 1)]
        backward = [(target, source) for source, target in forward]
        low = lax.ppermute(
            lax.slice_in_dim(block, block.shape[dim] - width, None, axis=dim), axis, forward
        )
        high = lax.ppermute(lax.slice_in_dim(block, 0, width, axis=dim), axis, backward)
        block = jnp.concatenate([low, block, high], axis=dim)
    return block


def silu_slope(values):
    logistic = jax.nn.sigmoid(values)
    return logistic * (1.0 + values * (1.0 - logistic))


def widen_cols(values):
    return jnp.pad(values, ((0, 0), (0, 0), (1, 1), (0, 0)))


def tap_columns(padded, frames, height, across):
    pieces = []
    for time_tap in range(3):
        for row_tap in range(3):
            for col_tap in range(3):
                start_time, start_row, start_col = (2 - time_tap, 2 - row_tap, 2 - col_tap)
                pieces.append(
                    padded[
                        start_time : start_time + frames,
                        start_row : start_row + height,
                        start_col : start_col + across,
                    ]
                )
    stacked = jnp.stack(pieces, 3)
    return stacked.reshape(frames * height * across, 27, padded.shape[3])


def backward_piece(columns, portion):
    return lax.dot_general(
        columns, portion, (((1, 2), (0, 2)), ((), ())), preferred_element_type=jnp.float32
    )


def kernel_grad(haloed, gradient, factor):
    height = gradient.shape[1]
    across = gradient.shape[2]
    channels = haloed.shape[3]
    split_grads = lax.all_to_all(gradient, "tm", split_axis=3, concat_axis=0, tiled=True)
    width_out = split_grads.shape[3]
    padded_grads = jnp.pad(split_grads, ((0, 2), (0, 0), (0, 0), (0, 0)))
    portion = lax.all_gather(haloed, "tm", axis=0, tiled=True)
    offset = jnp.int32(0)
    portion_frames = portion.shape[0]
    widened = widen_cols(portion)
    spatial = jnp.stack(
        [
            widened[:, row_tap : row_tap + height, col_tap : col_tap + across]
            for row_tap in range(3)
            for col_tap in range(3)
        ],
        3,
    )
    shifted_grads = jnp.stack(
        [
            lax.dynamic_slice_in_dim(padded_grads, offset + 2 - time_tap, portion_frames, 0)
            for time_tap in range(3)
        ],
        0,
    )
    contribution = lax.dot_general(
        spatial,
        shifted_grads,
        (((0, 1, 2), (1, 2, 3)), ((), ())),
        preferred_element_type=jnp.float32,
    )
    contribution = jnp.transpose(contribution, (2, 0, 1, 3)).reshape(27, channels, width_out)
    return lax.psum_scatter(contribution * factor, "rows", scatter_dimension=1, tiled=True)


def gathered_plan(inputs, cotangent, kernel):
    frames, height, across, channels = inputs.shape
    positions = frames * height * across
    rows_kernel = lax.all_gather(kernel, "rows", axis=1, tiled=True)
    act = jax.nn.silu(inputs.astype(jnp.float32)).astype(jnp.bfloat16)
    paired = jnp.concatenate([act, cotangent], 3)
    paired_rows = extended(paired, (("rows", 1),), 1)
    halo_act = paired_rows[:, :, :, :channels]
    halo_grad = paired_rows[:, :, :, channels:]
    split_bands = lax.all_to_all(halo_grad, "tm", split_axis=3, concat_axis=0, tiled=True)
    total_frames = split_bands.shape[0]
    padded_bands = jnp.pad(split_bands, ((0, 2), (0, 0), (0, 0), (0, 0)))
    cols_all = tap_columns(widen_cols(padded_bands), total_frames, height, across)
    partial_terms = backward_piece(cols_all, rows_kernel).reshape(
        total_frames // frames, positions, channels
    )
    grad_act = lax.psum_scatter(partial_terms, "tm", scatter_dimension=0, tiled=True)
    grad_act = grad_act.reshape(frames, height, across, channels)
    grad_inputs = (
        cotangent.astype(jnp.float32) + grad_act * silu_slope(inputs.astype(jnp.float32))
    ).astype(jnp.bfloat16)
    factor = float(frames * lax.axis_size("tm") * height * lax.axis_size("rows") * across) ** (-0.5)
    grad_kernel = kernel_grad(halo_act, cotangent, factor)
    return (grad_inputs, grad_kernel)


def exchange_fits(inputs, cotangent, kernel):
    frames, height, across, channels = inputs.shape
    groups, bands = lax.axis_size("tm"), lax.axis_size("rows")
    own_in, own_out = kernel.shape[1], kernel.shape[2]
    return (
        frames == 2
        and frames * height * across == LANES
        and across == 16
        and own_in == 16
        and own_out == LANES
        and groups == 2
        and bands % 8 == 0
        and channels == own_in * bands == own_out * groups
        and frames * groups * height * bands * across * own_out * 2 <= 4 * 2**20
    )


def exchange_kernel(
    groups, bands, factor,
    inputs_ref, cot_ref, kernel_ref, grad_in_ref, grad_kernel_ref,
    grads, acts, act_send, back_send, back, spatial,
    ring_recv, pair_recv, ring_send, core_send, core_recv, own_sem,
    act_send_sem, act_recv_sem, back_send_sem, back_recv_sem,
):
    frames, height, across, channels = inputs_ref.shape
    own_in = kernel_ref.shape[1]
    positions = frames * height * across
    rows = height * bands
    plane = rows * across
    all_frames = frames * groups
    devices = groups * bands
    chips = bands // 2
    half = LANES // 2

    group, band = lax.axis_index("tm"), lax.axis_index("rows")
    me = group * bands + band
    chip, core = band // 2, band % 2
    column = chip % 2
    place = (1 - column) * (chip // 2) + column * (chips - 1 - chip // 2)

    def band_at(spot):
        spot = (spot + chips) % chips
        side = spot // (chips // 2)
        at = (1 - side) * (2 * spot) + side * (2 * (chips - 1 - spot) + 1)
        return at * 2 + core

    def device(index):
        return (index // bands, index % bands)

    def region(group_of, band_of):
        return grads.at[pl.ds(group_of * frames, frames), pl.ds(band_of * height, height)]

    def wait_bytes(ref, sem):
        pltpu.make_async_copy(ref, ref, sem).wait()

    barrier = pltpu.get_barrier_semaphore()

    def greet(step, carry):
        pl.semaphore_signal(
            barrier, inc=1, device_id=device((me + step) % devices), device_id_type=MESH
        )
        return carry

    lax.fori_loop(1, devices, greet, 0)

    values = inputs_ref[...].reshape(positions, channels).astype(jnp.float32)
    act = values * jax.nn.sigmoid(values)
    act_send[...] = act.T.astype(jnp.bfloat16).reshape(bands, own_in, positions)

    pl.semaphore_wait(barrier, devices - 1)

    partner = (group + 1) % groups
    own_part = cot_ref.at[:, :, :, pl.ds(pl.multiple_of(group * LANES, LANES), LANES)]
    other_part = cot_ref.at[:, :, :, pl.ds(pl.multiple_of(partner * LANES, LANES), LANES)]
    pltpu.make_async_remote_copy(
        src_ref=other_part, dst_ref=region(group, band), send_sem=ring_send, recv_sem=pair_recv,
        device_id=(partner, band), device_id_type=MESH,
    ).start()

    def top_hop(way, piece):
        return chips // 2 if way == piece else chips // 2 - 1

    def forward(source, piece, way, hop, band_of):
        target = band_at(place + 1) if way == 0 else band_at(place - 1)
        pltpu.make_async_remote_copy(
            src_ref=source, dst_ref=region((group + piece) % groups, band_of),
            send_sem=ring_send, recv_sem=ring_recv.at[way, hop - 1, piece],
            device_id=(group, target), device_id_type=MESH,
        ).start()

    def to_other_core(source, piece, band_of):
        pltpu.make_async_remote_copy(
            src_ref=source, dst_ref=region((group + piece) % groups, band_of),
            send_sem=core_send, recv_sem=core_recv,
            device_id=(group, chip * 2 + 1 - core), device_id_type=MESH,
        ).start()

    def send_act(step, carry):
        target = (me + step) % devices
        pltpu.make_async_remote_copy(
            src_ref=act_send.at[target % bands], dst_ref=acts.at[me],
            send_sem=act_send_sem, recv_sem=act_recv_sem,
            device_id=device(target), device_id_type=MESH,
        ).start()
        return carry

    for way in range(2):
        forward(own_part, 0, way, 1, band)
    to_other_core(own_part, 0, band)
    own_copy = pltpu.make_async_copy(own_part, region(group, band), own_sem)
    own_copy.start()
    own_act = pltpu.make_async_copy(act_send.at[band], acts.at[me], act_recv_sem)
    own_act.start()

    wait_bytes(region(partner, band), pair_recv)
    for way in range(2):
        forward(region(partner, band), 1, way, 1, band)
    to_other_core(region(partner, band), 1, band)

    hops = chips // 2
    share = devices // hops
    for hop in range(1, hops + 1):
        first, last = max(1, (hop - 1) * share), devices if hop == hops else hop * share
        lax.fori_loop(first, last, send_act, 0)
        for piece in range(groups):
            for way in range(2):
                if hop > top_hop(way, piece):
                    continue
                band_of = band_at(place - hop if way == 0 else place + hop)
                arrived = region((group + piece) % groups, band_of)
                wait_bytes(arrived, ring_recv.at[way, hop - 1, piece])
                if hop < top_hop(way, piece):
                    forward(arrived, piece, way, hop + 1, band_of)
                to_other_core(arrived, piece, band_of)

    own_copy.wait()
    wait_bytes(grads.at[:, pl.ds(0, rows // 2)], core_recv)

    lane = lax.broadcasted_iota(jnp.int32, (own_in, plane), 1)
    col, row = lane % across, lane // across
    low = lax.broadcasted_iota(jnp.int32, (own_in, LANES), 1) < half

    def moved(block, by_row, by_col):
        shift = by_row * across + by_col
        if shift == 0:
            return block
        block = pltpu.roll(block, (-shift) % plane, 1)
        inside = None
        if by_row:
            inside = (row + by_row >= 0) & (row + by_row < rows)
        if by_col:
            in_cols = (col + by_col >= 0) & (col + by_col < across)
            inside = in_cols if inside is None else inside & in_cols
        return jnp.where(inside, block, 0.0)

    def taps_of(time_tap):
        return kernel_ref[pl.ds(9 * time_tap, 9)].reshape(9 * own_in, LANES)

    def grads_of(frame):
        return grads[frame].reshape(plane, LANES)

    def grad_act_of(frame):
        sums = None
        for time_tap in range(3):
            if frame + 2 - time_tap >= all_frames:
                continue
            term = lax.dot_general(
                taps_of(time_tap), grads_of(frame + 2 - time_tap),
                (((1,), (1,)), ((), ())), preferred_element_type=jnp.float32,
            )
            sums = term if sums is None else sums + term
        result = jnp.zeros((own_in, plane), jnp.float32)
        for col_tap in range(3):
            part = None
            for row_tap in range(3):
                tap = 3 * row_tap + col_tap
                term = moved(sums[tap * own_in : (tap + 1) * own_in], 1 - row_tap, 0)
                part = term if part is None else part + term
            result = result + moved(part, 0, 1 - col_tap)
        return result

    def send_back(step, carry):
        target = (me + step) % devices
        pltpu.make_async_remote_copy(
            src_ref=back_send.at[target], dst_ref=back.at[me],
            send_sem=back_send_sem, recv_sem=back_recv_sem,
            device_id=device(target), device_id_type=MESH,
        ).start()
        return carry

    for group_of in reversed(range(groups)):
        first = grad_act_of(group_of * frames)
        second = grad_act_of(group_of * frames + 1)
        for pair in range(bands // 2):
            x = first[:, pair * LANES : (pair + 1) * LANES]
            y = second[:, pair * LANES : (pair + 1) * LANES]
            back_send[group_of * bands + 2 * pair] = jnp.where(low, x, pltpu.roll(y, half, 1))
            back_send[group_of * bands + 2 * pair + 1] = jnp.where(low, pltpu.roll(x, half, 1), y)
    own_back = pltpu.make_async_copy(back_send.at[me], back.at[me], back_recv_sem)
    own_back.start()
    lax.fori_loop(1, devices, send_back, 0)

    wait_bytes(acts, act_recv_sem)
    for frame in range(all_frames):
        group_of, part = frame // frames, frame % frames
        tiles = []
        for pair in range(bands // 2):
            x = acts[group_of * bands + 2 * pair].astype(jnp.float32)
            y = acts[group_of * bands + 2 * pair + 1].astype(jnp.float32)
            if part == 0:
                tiles.append(jnp.where(low, x, pltpu.roll(y, half, 1)))
            else:
                tiles.append(jnp.where(low, pltpu.roll(x, half, 1), y))
        whole = jnp.concatenate(tiles, axis=1)
        for col_tap in range(3):
            shifted = moved(whole, 0, col_tap - 1)
            for row_tap in range(3):
                tap = 3 * row_tap + col_tap
                spatial[frame, pl.ds(tap * own_in, own_in)] = moved(
                    shifted, row_tap - 1, 0
                ).astype(jnp.bfloat16)
    for time_tap in range(3):
        sums = None
        for frame in range(2 - time_tap, all_frames):
            term = lax.dot_general(
                spatial[frame + time_tap - 2], grads_of(frame),
                (((1,), (0,)), ((), ())), preferred_element_type=jnp.float32,
            )
            sums = term if sums is None else sums + term
        grad_kernel_ref[pl.ds(9 * time_tap, 9)] = (sums * factor).reshape(9, own_in, LANES)

    wait_bytes(back, back_recv_sem)
    grad_act = back[pl.ds(0, bands)]
    for group_of in range(1, groups):
        grad_act = grad_act + back[pl.ds(group_of * bands, bands)]
    grad_act = grad_act.reshape(channels, positions).T
    cot = cot_ref[...].reshape(positions, channels).astype(jnp.float32)
    grad_in = cot + grad_act * silu_slope(values)
    grad_in_ref[...] = grad_in.astype(jnp.bfloat16).reshape(grad_in_ref.shape)

    pieces = 2 * (chips - 1) + groups - 1
    wait_bytes(grads.at[pl.ds(0, frames), pl.ds(0, height * pieces)], ring_send)
    wait_bytes(grads.at[:, pl.ds(0, rows // 2)], core_send)
    wait_bytes(acts.at[pl.ds(0, devices - 1)], act_send_sem)
    wait_bytes(back.at[pl.ds(0, devices - 1)], back_send_sem)


def exchange_plan(inputs, cotangent, kernel):
    frames, height, across, channels = inputs.shape
    taps, own_in, own_out = kernel.shape
    groups, bands = lax.axis_size("tm"), lax.axis_size("rows")
    positions = frames * height * across
    all_frames, rows, devices = frames * groups, height * bands, groups * bands
    factor = float(all_frames * rows * across) ** (-0.5)
    dma = pltpu.SemaphoreType.DMA
    return pl.pallas_call(
        functools.partial(exchange_kernel, groups, bands, factor),
        out_shape=(
            jax.ShapeDtypeStruct(inputs.shape, jnp.bfloat16),
            jax.ShapeDtypeStruct(kernel.shape, jnp.float32),
        ),
        in_specs=[pl.BlockSpec(memory_space=pltpu.VMEM)] * 3,
        out_specs=[pl.BlockSpec(memory_space=pltpu.VMEM)] * 2,
        scratch_shapes=[
            pltpu.VMEM((all_frames, rows, across, own_out), jnp.bfloat16),
            pltpu.VMEM((devices, own_in, positions), jnp.bfloat16),
            pltpu.VMEM((bands, own_in, positions), jnp.bfloat16),
            pltpu.VMEM((devices, own_in, positions), jnp.float32),
            pltpu.VMEM((devices, own_in, positions), jnp.float32),
            pltpu.VMEM((all_frames, 9 * own_in, rows * across), jnp.bfloat16),
            dma((2, bands // 4, groups)),
            dma,
            dma,
            dma,
            dma,
            dma,
            dma,
            dma,
            dma,
            dma,
        ],
        compiler_params=pltpu.CompilerParams(
            collective_id=0, has_side_effects=True, vmem_limit_bytes=40 * 2**20
        ),
    )(inputs, cotangent, kernel)


def local(inputs, cotangent, kernel):
    if exchange_fits(inputs, cotangent, kernel):
        return exchange_plan(inputs, cotangent, kernel)
    return gathered_plan(inputs, cotangent, kernel)


def solution(mesh):
    return jax.shard_map(
        local,
        mesh=mesh,
        in_specs=(P("tm", "rows", None, None), P("tm", "rows", None, None), P(None, "rows", "tm")),
        out_specs=(P("tm", "rows", None, None), P(None, "rows", "tm")),
        check_vma=False,
    )
```

```python
import functools

import jax
import jax.numpy as jnp
from jax import lax
from jax.experimental import pallas as pl
from jax.experimental.pallas import tpu as pltpu
from jax.sharding import PartitionSpec as P

MESH = pl.DeviceIdType.MESH
LANES = 128


def extended(block, sides, width):
    for axis, dim in sides:
        count = lax.axis_size(axis)
        forward = [(i, i + 1) for i in range(count - 1)]
        backward = [(target, source) for source, target in forward]
        low = lax.ppermute(
            lax.slice_in_dim(block, block.shape[dim] - width, None, axis=dim), axis, forward
        )
        high = lax.ppermute(lax.slice_in_dim(block, 0, width, axis=dim), axis, backward)
        block = jnp.concatenate([low, block, high], axis=dim)
    return block


def silu_slope(values):
    logistic = jax.nn.sigmoid(values)
    return logistic * (1.0 + values * (1.0 - logistic))


def widen_cols(values):
    return jnp.pad(values, ((0, 0), (0, 0), (1, 1), (0, 0)))


def tap_columns(padded, frames, height, across):
    pieces = []
    for time_tap in range(3):
        for row_tap in range(3):
            for col_tap in range(3):
                start_time, start_row, start_col = (2 - time_tap, 2 - row_tap, 2 - col_tap)
                pieces.append(
                    padded[
                        start_time : start_time + frames,
                        start_row : start_row + height,
                        start_col : start_col + across,
                    ]
                )
    stacked = jnp.stack(pieces, 3)
    return stacked.reshape(frames * height * across, 27, padded.shape[3])


def backward_piece(columns, portion):
    return lax.dot_general(
        columns, portion, (((1, 2), (0, 2)), ((), ())), preferred_element_type=jnp.float32
    )


def kernel_grad(haloed, gradient, factor):
    height = gradient.shape[1]
    across = gradient.shape[2]
    channels = haloed.shape[3]
    split_grads = lax.all_to_all(gradient, "tm", split_axis=3, concat_axis=0, tiled=True)
    width_out = split_grads.shape[3]
    padded_grads = jnp.pad(split_grads, ((0, 2), (0, 0), (0, 0), (0, 0)))
    portion = lax.all_gather(haloed, "tm", axis=0, tiled=True)
    offset = jnp.int32(0)
    portion_frames = portion.shape[0]
    widened = widen_cols(portion)
    spatial = jnp.stack(
        [
            widened[:, row_tap : row_tap + height, col_tap : col_tap + across]
            for row_tap in range(3)
            for col_tap in range(3)
        ],
        3,
    )
    shifted_grads = jnp.stack(
        [
            lax.dynamic_slice_in_dim(padded_grads, offset + 2 - time_tap, portion_frames, 0)
            for time_tap in range(3)
        ],
        0,
    )
    contribution = lax.dot_general(
        spatial,
        shifted_grads,
        (((0, 1, 2), (1, 2, 3)), ((), ())),
        preferred_element_type=jnp.float32,
    )
    contribution = jnp.transpose(contribution, (2, 0, 1, 3)).reshape(27, channels, width_out)
    return lax.psum_scatter(contribution * factor, "rows", scatter_dimension=1, tiled=True)


def gathered_plan(inputs, cotangent, kernel):
    frames, height, across, channels = inputs.shape
    positions = frames * height * across
    rows_kernel = lax.all_gather(kernel, "rows", axis=1, tiled=True)
    act = jax.nn.silu(inputs.astype(jnp.float32)).astype(jnp.bfloat16)
    paired = jnp.concatenate([act, cotangent], 3)
    paired_rows = extended(paired, (("rows", 1),), 1)
    halo_act = paired_rows[:, :, :, :channels]
    halo_grad = paired_rows[:, :, :, channels:]
    split_bands = lax.all_to_all(halo_grad, "tm", split_axis=3, concat_axis=0, tiled=True)
    total_frames = split_bands.shape[0]
    padded_bands = jnp.pad(split_bands, ((0, 2), (0, 0), (0, 0), (0, 0)))
    cols_all = tap_columns(widen_cols(padded_bands), total_frames, height, across)
    partial_terms = backward_piece(cols_all, rows_kernel).reshape(
        total_frames // frames, positions, channels
    )
    grad_act = lax.psum_scatter(partial_terms, "tm", scatter_dimension=0, tiled=True)
    grad_act = grad_act.reshape(frames, height, across, channels)
    grad_inputs = (
        cotangent.astype(jnp.float32) + grad_act * silu_slope(inputs.astype(jnp.float32))
    ).astype(jnp.bfloat16)
    factor = float(frames * lax.axis_size("tm") * height * lax.axis_size("rows") * across) ** (-0.5)
    grad_kernel = kernel_grad(halo_act, cotangent, factor)
    return (grad_inputs, grad_kernel)


def exchange_fits(inputs, cotangent, kernel):
    frames, height, across, channels = inputs.shape
    groups, bands = lax.axis_size("tm"), lax.axis_size("rows")
    own_in, own_out = kernel.shape[1], kernel.shape[2]
    return (
        frames == 2
        and frames * height * across == LANES
        and across == 16
        and own_in == 16
        and own_out == LANES
        and groups == 2
        and bands % 8 == 0
        and channels == own_in * bands == own_out * groups
        and frames * groups * height * bands * across * own_out * 2 <= 4 * 2**20
    )


def exchange_kernel(
    groups, bands, factor,
    inputs_hbm, cot_hbm, kernel_hbm, grad_in_ref, grad_kernel_ref,
    inputs_ref, cot_ref, kernel_ref, grads, acts, act_send, sums, part_send, part, back_send, back,
    spatial, load_sem, ring_recv, pair_recv, core_recv, ring_send, core_send, own_sem,
    act_send_sem, act_recv_sem, cross_send_sem, cross_recv_sem, part_send_sem, part_recv_sem,
    back_send_sem, back_recv_sem,
):
    frames, height, across, channels = inputs_ref.shape
    own_in = kernel_ref.shape[1]
    positions = frames * height * across
    rows = height * bands
    plane = rows * across
    all_frames = frames * groups
    chips = bands // 2
    hops = chips // 2
    half = LANES // 2

    group, band = lax.axis_index("tm"), lax.axis_index("rows")
    partner = (group + 1) % groups
    chip, core = band // 2, band % 2
    column = chip % 2
    place = (1 - column) * (chip // 2) + column * (chips - 1 - chip // 2)

    def chip_at(spot):
        spot = (spot + chips) % chips
        side = spot // (chips // 2)
        return (1 - side) * (2 * spot) + side * (2 * (chips - 1 - spot) + 1)

    def region(group_of, band_of):
        return grads.at[pl.ds(group_of * frames, frames), pl.ds(band_of * height, height)]

    def wait_bytes(ref, sem):
        pltpu.make_async_copy(ref, ref, sem).wait()

    barrier = pltpu.get_barrier_semaphore()

    def greet(step, carry):
        pl.semaphore_signal(
            barrier, inc=1, device_id=(group, (band + step) % bands), device_id_type=MESH
        )
        return carry

    lax.fori_loop(1, bands, greet, 0)
    pl.semaphore_signal(barrier, inc=1, device_id=(partner, band), device_id_type=MESH)

    load_inputs = pltpu.make_async_copy(inputs_hbm, inputs_ref, load_sem.at[0])
    load_cot = pltpu.make_async_copy(cot_hbm, cot_ref, load_sem.at[1])
    load_kernel = pltpu.make_async_copy(kernel_hbm, kernel_ref, load_sem.at[2])
    load_inputs.start()
    load_cot.start()
    load_kernel.start()

    load_inputs.wait()
    values = inputs_ref[...].reshape(positions, channels).astype(jnp.float32)
    act = values * jax.nn.sigmoid(values)
    act_send[...] = act.T.astype(jnp.bfloat16).reshape(bands, own_in, positions)
    load_cot.wait()

    pl.semaphore_wait(barrier, bands)

    own_part = cot_ref.at[:, :, :, pl.ds(pl.multiple_of(group * LANES, LANES), LANES)]
    other_part = cot_ref.at[:, :, :, pl.ds(pl.multiple_of(partner * LANES, LANES), LANES)]
    pltpu.make_async_remote_copy(
        src_ref=other_part, dst_ref=region(group, band), send_sem=ring_send, recv_sem=pair_recv,
        device_id=(partner, band), device_id_type=MESH,
    ).start()

    def top_hop(way, piece):
        return hops if way == piece else hops - 1

    def forward(source, piece, way, hop, band_of):
        target = chip_at(place + 1 if way == 0 else place - 1) * 2 + core
        pltpu.make_async_remote_copy(
            src_ref=source, dst_ref=region((group + piece) % groups, band_of),
            send_sem=ring_send, recv_sem=ring_recv.at[way, hop - 1, piece],
            device_id=(group, target), device_id_type=MESH,
        ).start()

    def to_other_core(source, piece, way, hop, band_of):
        pltpu.make_async_remote_copy(
            src_ref=source, dst_ref=region((group + piece) % groups, band_of),
            send_sem=core_send, recv_sem=core_recv.at[way, hop, piece],
            device_id=(group, chip * 2 + 1 - core), device_id_type=MESH,
        ).start()

    def send_act(step, carry):
        target = (band + step) % bands
        pltpu.make_async_remote_copy(
            src_ref=act_send.at[target], dst_ref=acts.at[group, band],
            send_sem=act_send_sem, recv_sem=act_recv_sem,
            device_id=(group, target), device_id_type=MESH,
        ).start()
        return carry

    for way in range(2):
        forward(own_part, 0, way, 1, band)
    to_other_core(own_part, 0, 0, 0, band)
    own_copy = pltpu.make_async_copy(own_part, region(group, band), own_sem)
    own_copy.start()
    own_act = pltpu.make_async_copy(act_send.at[band], acts.at[group, band], act_recv_sem)
    own_act.start()
    lax.fori_loop(1, bands, send_act, 0)

    wait_bytes(region(partner, band), pair_recv)
    for way in range(2):
        forward(region(partner, band), 1, way, 1, band)
    to_other_core(region(partner, band), 1, 0, 0, band)

    def pass_on(hop):
        for piece in range(groups):
            for way in range(2):
                if hop > top_hop(way, piece):
                    continue
                band_of = chip_at(place - hop if way == 0 else place + hop) * 2 + core
                arrived = region((group + piece) % groups, band_of)
                wait_bytes(arrived, ring_recv.at[way, hop - 1, piece])
                if hop < top_hop(way, piece):
                    forward(arrived, piece, way, hop + 1, band_of)
                to_other_core(arrived, piece, way, hop, band_of)

    lane = lax.broadcasted_iota(jnp.int32, (own_in, plane), 1)
    col, row = lane % across, lane // across
    low = lax.broadcasted_iota(jnp.int32, (own_in, LANES), 1) < half

    def moved(block, by_row, by_col):
        shift = by_row * across + by_col
        if shift == 0:
            return block
        block = pltpu.roll(block, (-shift) % plane, 1)
        inside = None
        if by_row:
            inside = (row + by_row >= 0) & (row + by_row < rows)
        if by_col:
            in_cols = (col + by_col >= 0) & (col + by_col < across)
            inside = in_cols if inside is None else inside & in_cols
        return jnp.where(inside, block, 0.0)

    def sum_taps(chip_of):
        taps = jnp.concatenate(
            [kernel_ref[pl.ds(9 * tap, 9)].reshape(9 * own_in, LANES) for tap in range(3)], axis=1
        )
        cells = [
            grads[frame, pl.ds(chip_of * 2 * height, 2 * height)].reshape(LANES, LANES)
            for frame in range(all_frames)
        ]
        for frame in range(all_frames):
            first = max(0, frame + 3 - all_frames)
            window = jnp.concatenate(
                [cells[frame + 2 - tap] for tap in range(first, 3)], axis=1
            )
            sums[chip_of, frame] = lax.dot_general(
                taps[:, first * LANES :], window, (((1,), (1,)), ((), ())),
                preferred_element_type=jnp.float32,
            )

    def sum_hop(hop):
        for way in range(2):
            chip_of = chip_at(place - hop if way == 0 else place + hop)
            if hop in (0, hops) and way == 1:
                continue
            for piece in range(groups):
                source_way = piece if hop == hops else way
                arrived = region((group + piece) % groups, chip_of * 2 + 1 - core)
                wait_bytes(arrived, core_recv.at[source_way, hop, piece])
            sum_taps(chip_of)

    pass_on(1)
    own_copy.wait()
    load_kernel.wait()
    sum_hop(0)

    pass_on(2)
    wait_bytes(acts.at[group], act_recv_sem)
    pltpu.make_async_remote_copy(
        src_ref=acts.at[group], dst_ref=acts.at[group],
        send_sem=cross_send_sem, recv_sem=cross_recv_sem,
        device_id=(partner, band), device_id_type=MESH,
    ).start()
    sum_hop(1)

    for hop in range(3, hops + 1):
        pass_on(hop)
        sum_hop(hop - 1)
    sum_hop(hops)

    def grad_act_of(frame):
        result = None
        for col_tap in range(3):
            mixed = None
            for row_tap in range(3):
                tap = 3 * row_tap + col_tap
                term = jnp.concatenate(
                    [sums[at, frame, pl.ds(tap * own_in, own_in)] for at in range(chips)], axis=1
                )
                term = moved(term, 1 - row_tap, 0)
                mixed = term if mixed is None else mixed + term
            mixed = moved(mixed, 0, 1 - col_tap)
            result = mixed if result is None else result + mixed
        return result

    for at in range(frames):
        part_send[at] = grad_act_of(partner * frames + at)
        pltpu.make_async_remote_copy(
            src_ref=part_send.at[at], dst_ref=part.at[at],
            send_sem=part_send_sem.at[at], recv_sem=part_recv_sem.at[at],
            device_id=(partner, band), device_id_type=MESH,
        ).start()
    own_share = [grad_act_of(group * frames + at) for at in range(frames)]
    for at in range(frames):
        wait_bytes(part.at[at], part_recv_sem.at[at])
    first, second = [own_share[at] + part[at] for at in range(frames)]
    for pair in range(bands // 2):
        x = first[:, pair * LANES : (pair + 1) * LANES]
        y = second[:, pair * LANES : (pair + 1) * LANES]
        back_send[2 * pair] = jnp.where(low, x, pltpu.roll(y, half, 1))
        back_send[2 * pair + 1] = jnp.where(low, pltpu.roll(x, half, 1), y)

    def send_back(step, carry):
        target = (band + step) % bands
        pltpu.make_async_remote_copy(
            src_ref=back_send.at[target], dst_ref=back.at[band],
            send_sem=back_send_sem, recv_sem=back_recv_sem,
            device_id=(group, target), device_id_type=MESH,
        ).start()
        return carry

    lax.fori_loop(1, bands, send_back, 0)
    own_back = pltpu.make_async_copy(back_send.at[band], back.at[band], back_recv_sem)
    own_back.start()

    wait_bytes(acts.at[partner], cross_recv_sem)
    for frame in range(all_frames):
        group_of, at = frame // frames, frame % frames
        tiles = []
        for pair in range(bands // 2):
            x = acts[group_of, 2 * pair].astype(jnp.float32)
            y = acts[group_of, 2 * pair + 1].astype(jnp.float32)
            if at == 0:
                tiles.append(jnp.where(low, x, pltpu.roll(y, half, 1)))
            else:
                tiles.append(jnp.where(low, pltpu.roll(x, half, 1), y))
        whole = jnp.concatenate(tiles, axis=1)
        for col_tap in range(3):
            shifted = moved(whole, 0, col_tap - 1)
            for row_tap in range(3):
                tap = 3 * row_tap + col_tap
                spatial[frame, pl.ds(tap * own_in, own_in)] = moved(
                    shifted, row_tap - 1, 0
                ).astype(jnp.bfloat16)
    for time_tap in range(3):
        total = None
        for frame in range(2 - time_tap, all_frames):
            term = lax.dot_general(
                spatial[frame + time_tap - 2], grads[frame].reshape(plane, LANES),
                (((1,), (0,)), ((), ())), preferred_element_type=jnp.float32,
            )
            total = term if total is None else total + term
        grad_kernel_ref[pl.ds(9 * time_tap, 9)] = (total * factor).reshape(9, own_in, LANES)

    wait_bytes(back, back_recv_sem)
    grad_act = back[...].reshape(channels, positions).T
    values = inputs_ref[...].reshape(positions, channels).astype(jnp.float32)
    cot = cot_ref[...].reshape(positions, channels).astype(jnp.float32)
    grad_in = cot + grad_act * silu_slope(values)
    grad_in_ref[...] = grad_in.astype(jnp.bfloat16).reshape(grad_in_ref.shape)

    pieces = 2 * (chips - 1) + 1
    wait_bytes(grads.at[pl.ds(0, frames), pl.ds(0, height * pieces)], ring_send)
    wait_bytes(grads.at[:, pl.ds(0, rows // 2)], core_send)
    wait_bytes(acts.at[0, pl.ds(0, bands - 1)], act_send_sem)
    wait_bytes(acts.at[group], cross_send_sem)
    for at in range(frames):
        wait_bytes(part_send.at[at], part_send_sem.at[at])
    wait_bytes(back.at[pl.ds(0, bands - 1)], back_send_sem)


def exchange_plan(inputs, cotangent, kernel):
    frames, height, across, channels = inputs.shape
    taps, own_in, own_out = kernel.shape
    groups, bands = lax.axis_size("tm"), lax.axis_size("rows")
    positions = frames * height * across
    all_frames, rows = frames * groups, height * bands
    chips, plane = bands // 2, rows * across
    factor = float(all_frames * plane) ** (-0.5)
    dma = pltpu.SemaphoreType.DMA
    bf16, f32 = jnp.bfloat16, jnp.float32
    return pl.pallas_call(
        functools.partial(exchange_kernel, groups, bands, factor),
        out_shape=(
            jax.ShapeDtypeStruct(inputs.shape, bf16),
            jax.ShapeDtypeStruct(kernel.shape, f32),
        ),
        in_specs=[pl.BlockSpec(memory_space=pltpu.HBM)] * 3,
        out_specs=[pl.BlockSpec(memory_space=pltpu.VMEM)] * 2,
        scratch_shapes=[
            pltpu.VMEM(inputs.shape, bf16),
            pltpu.VMEM(cotangent.shape, bf16),
            pltpu.VMEM(kernel.shape, bf16),
            pltpu.VMEM((all_frames, rows, across, own_out), bf16),
            pltpu.VMEM((groups, bands, own_in, positions), bf16),
            pltpu.VMEM((bands, own_in, positions), bf16),
            pltpu.VMEM((chips, all_frames, 9 * own_in, LANES), f32),
            pltpu.VMEM((frames, own_in, plane), f32),
            pltpu.VMEM((frames, own_in, plane), f32),
            pltpu.VMEM((bands, own_in, positions), f32),
            pltpu.VMEM((bands, own_in, positions), f32),
            pltpu.VMEM((all_frames, 9 * own_in, plane), bf16),
            dma((3,)),
            dma((2, chips // 2, groups)),
            dma,
            dma((2, chips // 2 + 1, groups)),
            dma,
            dma,
            dma,
            dma,
            dma,
            dma,
            dma,
            dma((frames,)),
            dma((frames,)),
            dma,
            dma,
        ],
        compiler_params=pltpu.CompilerParams(
            collective_id=0, has_side_effects=True, vmem_limit_bytes=40 * 2**20
        ),
    )(inputs, cotangent, kernel)


def local(inputs, cotangent, kernel):
    if exchange_fits(inputs, cotangent, kernel):
        return exchange_plan(inputs, cotangent, kernel)
    return gathered_plan(inputs, cotangent, kernel)


def solution(mesh):
    return jax.shard_map(
        local,
        mesh=mesh,
        in_specs=(P("tm", "rows", None, None), P("tm", "rows", None, None), P(None, "rows", "tm")),
        out_specs=(P("tm", "rows", None, None), P(None, "rows", "tm")),
        check_vma=False,
    )
```

```python
import functools

import jax
import jax.numpy as jnp
from jax import lax
from jax.experimental import pallas as pl
from jax.experimental.pallas import tpu as pltpu
from jax.sharding import PartitionSpec as P

MESH = pl.DeviceIdType.MESH
LANES = 128


def extended(block, sides, width):
    for axis, dim in sides:
        count = lax.axis_size(axis)
        forward = [(i, i + 1) for i in range(count - 1)]
        backward = [(target, source) for source, target in forward]
        low = lax.ppermute(
            lax.slice_in_dim(block, block.shape[dim] - width, None, axis=dim), axis, forward
        )
        high = lax.ppermute(lax.slice_in_dim(block, 0, width, axis=dim), axis, backward)
        block = jnp.concatenate([low, block, high], axis=dim)
    return block


def silu_slope(values):
    logistic = jax.nn.sigmoid(values)
    return logistic * (1.0 + values * (1.0 - logistic))


def widen_cols(values):
    return jnp.pad(values, ((0, 0), (0, 0), (1, 1), (0, 0)))


def tap_columns(padded, frames, height, across):
    pieces = []
    for time_tap in range(3):
        for row_tap in range(3):
            for col_tap in range(3):
                start_time, start_row, start_col = (2 - time_tap, 2 - row_tap, 2 - col_tap)
                pieces.append(
                    padded[
                        start_time : start_time + frames,
                        start_row : start_row + height,
                        start_col : start_col + across,
                    ]
                )
    stacked = jnp.stack(pieces, 3)
    return stacked.reshape(frames * height * across, 27, padded.shape[3])


def backward_piece(columns, portion):
    return lax.dot_general(
        columns, portion, (((1, 2), (0, 2)), ((), ())), preferred_element_type=jnp.float32
    )


def kernel_grad(haloed, gradient, factor):
    height = gradient.shape[1]
    across = gradient.shape[2]
    channels = haloed.shape[3]
    split_grads = lax.all_to_all(gradient, "tm", split_axis=3, concat_axis=0, tiled=True)
    width_out = split_grads.shape[3]
    padded_grads = jnp.pad(split_grads, ((0, 2), (0, 0), (0, 0), (0, 0)))
    portion = lax.all_gather(haloed, "tm", axis=0, tiled=True)
    offset = jnp.int32(0)
    portion_frames = portion.shape[0]
    widened = widen_cols(portion)
    spatial = jnp.stack(
        [
            widened[:, row_tap : row_tap + height, col_tap : col_tap + across]
            for row_tap in range(3)
            for col_tap in range(3)
        ],
        3,
    )
    shifted_grads = jnp.stack(
        [
            lax.dynamic_slice_in_dim(padded_grads, offset + 2 - time_tap, portion_frames, 0)
            for time_tap in range(3)
        ],
        0,
    )
    contribution = lax.dot_general(
        spatial,
        shifted_grads,
        (((0, 1, 2), (1, 2, 3)), ((), ())),
        preferred_element_type=jnp.float32,
    )
    contribution = jnp.transpose(contribution, (2, 0, 1, 3)).reshape(27, channels, width_out)
    return lax.psum_scatter(contribution * factor, "rows", scatter_dimension=1, tiled=True)


def gathered_plan(inputs, cotangent, kernel):
    frames, height, across, channels = inputs.shape
    positions = frames * height * across
    rows_kernel = lax.all_gather(kernel, "rows", axis=1, tiled=True)
    act = jax.nn.silu(inputs.astype(jnp.float32)).astype(jnp.bfloat16)
    paired = jnp.concatenate([act, cotangent], 3)
    paired_rows = extended(paired, (("rows", 1),), 1)
    halo_act = paired_rows[:, :, :, :channels]
    halo_grad = paired_rows[:, :, :, channels:]
    split_bands = lax.all_to_all(halo_grad, "tm", split_axis=3, concat_axis=0, tiled=True)
    total_frames = split_bands.shape[0]
    padded_bands = jnp.pad(split_bands, ((0, 2), (0, 0), (0, 0), (0, 0)))
    cols_all = tap_columns(widen_cols(padded_bands), total_frames, height, across)
    partial_terms = backward_piece(cols_all, rows_kernel).reshape(
        total_frames // frames, positions, channels
    )
    grad_act = lax.psum_scatter(partial_terms, "tm", scatter_dimension=0, tiled=True)
    grad_act = grad_act.reshape(frames, height, across, channels)
    grad_inputs = (
        cotangent.astype(jnp.float32) + grad_act * silu_slope(inputs.astype(jnp.float32))
    ).astype(jnp.bfloat16)
    factor = float(frames * lax.axis_size("tm") * height * lax.axis_size("rows") * across) ** (-0.5)
    grad_kernel = kernel_grad(halo_act, cotangent, factor)
    return (grad_inputs, grad_kernel)


def exchange_fits(inputs, cotangent, kernel):
    frames, height, across, channels = inputs.shape
    groups, bands = lax.axis_size("tm"), lax.axis_size("rows")
    own_in, own_out = kernel.shape[1], kernel.shape[2]
    return (
        frames == 2
        and frames * height * across == LANES
        and across == 16
        and own_in == 16
        and own_out == LANES
        and groups == 2
        and bands == 16
        and channels == own_in * bands == own_out * groups
        and frames * groups * height * bands * across * own_out * 2 <= 4 * 2**20
    )


def exchange_kernel(
    groups, bands, factor,
    inputs_hbm, cot_hbm, kernel_hbm, grad_in_hbm, grad_kernel_hbm,
    inputs_ref, cot_ref, kernel_ref, grad_in_ref, grad_kernel_ref, grads, acts, act_send, sums, part_send, part, back_send, back,
    spatial, load_sem, store_sem, line_recv, side_recv, core_recv, line_send, side_send, core_send, own_sem,
    act_send_sem, act_recv_sem, cross_send_sem, cross_recv_sem, part_send_sem, part_recv_sem,
    back_send_sem, back_recv_sem,
):
    frames, height, across, channels = inputs_ref.shape
    own_in = kernel_ref.shape[1]
    positions = frames * height * across
    rows = height * bands
    plane = rows * across
    all_frames = frames * groups
    chips = bands // 2
    depth = chips // 2
    half = LANES // 2

    group, band = lax.axis_index("tm"), lax.axis_index("rows")
    partner = (group + 1) % groups
    chip, core = band // 2, band % 2
    layer, column = chip // 2, chip % 2
    layers = [layer, layer + 1 - 2 * (layer % 2), 2 - layer // 2, 3 * (1 - layer // 2)]

    def chip_at(layer_of, column_of):
        return layer_of * 2 + column_of

    def region(group_of, band_of):
        return grads.at[pl.ds(group_of * frames, frames), pl.ds(band_of * height, height)]

    def wait_bytes(ref, sem):
        pltpu.make_async_copy(ref, ref, sem).wait()

    barrier = pltpu.get_barrier_semaphore()

    def greet(step, carry):
        pl.semaphore_signal(
            barrier, inc=1, device_id=(group, (band + step) % bands), device_id_type=MESH
        )
        return carry

    lax.fori_loop(1, bands, greet, 0)
    for layer_of in range(depth):
        pl.semaphore_signal(
            barrier, inc=1, device_id=(partner, chip_at(layer_of, column) * 2 + core),
            device_id_type=MESH,
        )

    load_inputs = pltpu.make_async_copy(inputs_hbm, inputs_ref, load_sem.at[0])
    load_cot = pltpu.make_async_copy(cot_hbm, cot_ref, load_sem.at[1])
    load_kernel = pltpu.make_async_copy(kernel_hbm, kernel_ref, load_sem.at[2])
    load_inputs.start()
    load_cot.start()
    load_kernel.start()

    load_cot.wait()
    pl.semaphore_wait(barrier, bands - 1 + depth)

    own_part = cot_ref.at[:, :, :, pl.ds(pl.multiple_of(group * LANES, LANES), LANES)]
    other_part = cot_ref.at[:, :, :, pl.ds(pl.multiple_of(partner * LANES, LANES), LANES)]

    def send_line(source, piece, layer_of):
        pltpu.make_async_remote_copy(
            src_ref=source, dst_ref=region(group, band),
            send_sem=line_send, recv_sem=line_recv.at[layer, piece],
            device_id=((group + piece) % groups, chip_at(layer_of, column) * 2 + core),
            device_id_type=MESH,
        ).start()

    def to_other_column(source, piece, layer_of):
        pltpu.make_async_remote_copy(
            src_ref=source,
            dst_ref=region((group + piece) % groups, chip_at(layer_of, column) * 2 + core),
            send_sem=side_send, recv_sem=side_recv.at[layer_of, piece],
            device_id=(group, chip_at(layer, 1 - column) * 2 + core), device_id_type=MESH,
        ).start()

    def to_other_core(source, piece, layer_of, side):
        column_of = column + side - 2 * column * side
        pltpu.make_async_remote_copy(
            src_ref=source,
            dst_ref=region((group + piece) % groups, chip_at(layer_of, column_of) * 2 + core),
            send_sem=core_send, recv_sem=core_recv.at[side, layer_of, piece],
            device_id=(group, chip * 2 + 1 - core), device_id_type=MESH,
        ).start()

    def send_act(step, carry):
        target = (band + step) % bands
        pltpu.make_async_remote_copy(
            src_ref=act_send.at[target], dst_ref=acts.at[group, band],
            send_sem=act_send_sem, recv_sem=act_recv_sem,
            device_id=(group, target), device_id_type=MESH,
        ).start()
        return carry

    for turn in range(1, depth):
        send_line(own_part, 0, layers[turn])
        send_line(other_part, 1, layers[turn])
        if turn == 1:
            to_other_column(own_part, 0, layer)
            send_line(other_part, 1, layer)
    to_other_core(own_part, 0, layer, 0)
    own_copy = pltpu.make_async_copy(own_part, region(group, band), own_sem)
    own_copy.start()

    load_inputs.wait()
    values = inputs_ref[...].reshape(positions, channels).astype(jnp.float32)
    act = values * jax.nn.sigmoid(values)
    act_send[...] = act.T.astype(jnp.bfloat16).reshape(bands, own_in, positions)
    own_act = pltpu.make_async_copy(act_send.at[band], acts.at[group, band], act_recv_sem)
    own_act.start()
    lax.fori_loop(1, bands, send_act, 0)

    def pass_line(turn):
        for piece in range(groups):
            if turn == 0 and piece == 0:
                continue
            layer_of = layers[turn]
            arrived = region((group + piece) % groups, chip_at(layer_of, column) * 2 + core)
            wait_bytes(arrived, line_recv.at[layer_of, piece])
            to_other_column(arrived, piece, layer_of)
            to_other_core(arrived, piece, layer_of, 0)

    def pass_side(turn):
        for piece in range(groups):
            layer_of = layers[turn]
            arrived = region((group + piece) % groups, chip_at(layer_of, 1 - column) * 2 + core)
            wait_bytes(arrived, side_recv.at[layer_of, piece])
            to_other_core(arrived, piece, layer_of, 1)

    lane = lax.broadcasted_iota(jnp.int32, (own_in, plane), 1)
    col, row = lane % across, lane // across
    low = lax.broadcasted_iota(jnp.int32, (own_in, LANES), 1) < half

    def moved(block, by_row, by_col):
        shift = by_row * across + by_col
        if shift == 0:
            return block
        block = pltpu.roll(block, (-shift) % plane, 1)
        inside = None
        if by_row:
            inside = (row + by_row >= 0) & (row + by_row < rows)
        if by_col:
            in_cols = (col + by_col >= 0) & (col + by_col < across)
            inside = in_cols if inside is None else inside & in_cols
        return jnp.where(inside, block, 0.0)

    def sum_taps(chip_of):
        taps = jnp.concatenate(
            [kernel_ref[pl.ds(9 * tap, 9)].reshape(9 * own_in, LANES) for tap in range(3)], axis=1
        )
        cells = [
            grads[frame, pl.ds(chip_of * 2 * height, 2 * height)].reshape(LANES, LANES)
            for frame in range(all_frames)
        ]
        for frame in range(all_frames):
            first = max(0, frame + 3 - all_frames)
            window = jnp.concatenate(
                [cells[frame + 2 - tap] for tap in range(first, 3)], axis=1
            )
            sums[chip_of, frame] = lax.dot_general(
                taps[:, first * LANES :], window, (((1,), (1,)), ((), ())),
                preferred_element_type=jnp.float32,
            )

    def sum_chip(turn, side):
        layer_of = layers[turn]
        chip_of = chip_at(layer_of, column + side - 2 * column * side)
        for piece in range(groups):
            arrived = region((group + piece) % groups, chip_of * 2 + 1 - core)
            wait_bytes(arrived, core_recv.at[side, layer_of, piece])
        sum_taps(chip_of)

    def shift_acts(group_of):
        for at in range(frames):
            tiles = []
            for pair in range(bands // 2):
                x = acts[group_of, 2 * pair].astype(jnp.float32)
                y = acts[group_of, 2 * pair + 1].astype(jnp.float32)
                if at == 0:
                    tiles.append(jnp.where(low, x, pltpu.roll(y, half, 1)))
                else:
                    tiles.append(jnp.where(low, pltpu.roll(x, half, 1), y))
            whole = jnp.concatenate(tiles, axis=1)
            for col_tap in range(3):
                shifted = moved(whole, 0, col_tap - 1)
                for row_tap in range(3):
                    tap = 3 * row_tap + col_tap
                    spatial[group_of * frames + at, pl.ds(tap * own_in, own_in)] = moved(
                        shifted, row_tap - 1, 0
                    ).astype(jnp.bfloat16)

    pass_line(0)
    pass_line(1)
    own_copy.wait()
    load_kernel.wait()
    pass_side(0)
    sum_chip(0, 0)
    pass_line(2)
    pass_side(1)
    wait_bytes(acts.at[group], act_recv_sem)
    pltpu.make_async_remote_copy(
        src_ref=acts.at[group], dst_ref=acts.at[group],
        send_sem=cross_send_sem, recv_sem=cross_recv_sem,
        device_id=(partner, band), device_id_type=MESH,
    ).start()
    sum_chip(1, 0)
    sum_chip(0, 1)
    pass_line(3)
    pass_side(2)
    shift_acts(group)
    sum_chip(2, 0)
    sum_chip(1, 1)
    pass_side(3)
    sum_chip(3, 0)
    sum_chip(2, 1)
    sum_chip(3, 1)

    def grad_act_of(frame):
        result = None
        for col_tap in range(3):
            mixed = None
            for row_tap in range(3):
                tap = 3 * row_tap + col_tap
                term = jnp.concatenate(
                    [sums[at, frame, pl.ds(tap * own_in, own_in)] for at in range(chips)], axis=1
                )
                term = moved(term, 1 - row_tap, 0)
                mixed = term if mixed is None else mixed + term
            mixed = moved(mixed, 0, 1 - col_tap)
            result = mixed if result is None else result + mixed
        return result

    for at in range(frames):
        part_send[at] = grad_act_of(partner * frames + at)
        pltpu.make_async_remote_copy(
            src_ref=part_send.at[at], dst_ref=part.at[at],
            send_sem=part_send_sem.at[at], recv_sem=part_recv_sem.at[at],
            device_id=(partner, band), device_id_type=MESH,
        ).start()
    own_share = [grad_act_of(group * frames + at) for at in range(frames)]

    wait_bytes(acts.at[partner], cross_recv_sem)
    shift_acts(partner)

    def kernel_taps(time_tap):
        total = None
        for frame in range(2 - time_tap, all_frames):
            term = lax.dot_general(
                spatial[frame + time_tap - 2], grads[frame].reshape(plane, LANES),
                (((1,), (0,)), ((), ())), preferred_element_type=jnp.float32,
            )
            total = term if total is None else total + term
        grad_kernel_ref[pl.ds(9 * time_tap, 9)] = (total * factor).reshape(9, own_in, LANES)
        own = pl.ds(9 * time_tap, 9)
        pltpu.make_async_copy(
            grad_kernel_ref.at[own], grad_kernel_hbm.at[own], store_sem.at[time_tap]
        ).start()

    kernel_taps(0)
    for at in range(frames):
        wait_bytes(part.at[at], part_recv_sem.at[at])
    first, second = [own_share[at] + part[at] for at in range(frames)]
    for pair in range(bands // 2):
        x = first[:, pair * LANES : (pair + 1) * LANES]
        y = second[:, pair * LANES : (pair + 1) * LANES]
        back_send[2 * pair] = jnp.where(low, x, pltpu.roll(y, half, 1))
        back_send[2 * pair + 1] = jnp.where(low, pltpu.roll(x, half, 1), y)

    def send_back(step, carry):
        target = (band + step) % bands
        pltpu.make_async_remote_copy(
            src_ref=back_send.at[target], dst_ref=back.at[band],
            send_sem=back_send_sem, recv_sem=back_recv_sem,
            device_id=(group, target), device_id_type=MESH,
        ).start()
        return carry

    lax.fori_loop(1, bands, send_back, 0)
    own_back = pltpu.make_async_copy(back_send.at[band], back.at[band], back_recv_sem)
    own_back.start()

    for time_tap in range(1, 3):
        kernel_taps(time_tap)

    wait_bytes(back, back_recv_sem)
    grad_act = back[...].reshape(channels, positions).T
    values = inputs_ref[...].reshape(positions, channels).astype(jnp.float32)
    cot = cot_ref[...].reshape(positions, channels).astype(jnp.float32)
    grad_in = cot + grad_act * silu_slope(values)
    grad_in_ref[...] = grad_in.astype(jnp.bfloat16).reshape(grad_in_ref.shape)
    store_in = pltpu.make_async_copy(grad_in_ref, grad_in_hbm, store_sem.at[3])
    store_in.start()

    line_rows = height * (2 * depth - 1)
    wait_bytes(grads.at[pl.ds(0, frames), pl.ds(0, line_rows)], line_send)
    wait_bytes(grads.at[pl.ds(0, frames), pl.ds(0, rows // 2)], side_send)
    wait_bytes(grads.at[:, pl.ds(0, rows // 2)], core_send)
    wait_bytes(acts.at[0, pl.ds(0, bands - 1)], act_send_sem)
    wait_bytes(acts.at[group], cross_send_sem)
    for at in range(frames):
        wait_bytes(part_send.at[at], part_send_sem.at[at])
    wait_bytes(back.at[pl.ds(0, bands - 1)], back_send_sem)
    for time_tap in range(3):
        own = pl.ds(9 * time_tap, 9)
        wait_bytes(grad_kernel_ref.at[own], store_sem.at[time_tap])
    store_in.wait()


def exchange_plan(inputs, cotangent, kernel):
    frames, height, across, channels = inputs.shape
    taps, own_in, own_out = kernel.shape
    groups, bands = lax.axis_size("tm"), lax.axis_size("rows")
    positions = frames * height * across
    all_frames, rows = frames * groups, height * bands
    chips, plane = bands // 2, rows * across
    factor = float(all_frames * plane) ** (-0.5)
    dma = pltpu.SemaphoreType.DMA
    bf16, f32 = jnp.bfloat16, jnp.float32
    return pl.pallas_call(
        functools.partial(exchange_kernel, groups, bands, factor),
        out_shape=(
            jax.ShapeDtypeStruct(inputs.shape, bf16),
            jax.ShapeDtypeStruct(kernel.shape, f32),
        ),
        in_specs=[pl.BlockSpec(memory_space=pltpu.HBM)] * 3,
        out_specs=[pl.BlockSpec(memory_space=pltpu.HBM)] * 2,
        scratch_shapes=[
            pltpu.VMEM(inputs.shape, bf16),
            pltpu.VMEM(cotangent.shape, bf16),
            pltpu.VMEM(kernel.shape, bf16),
            pltpu.VMEM(inputs.shape, bf16),
            pltpu.VMEM(kernel.shape, f32),
            pltpu.VMEM((all_frames, rows, across, own_out), bf16),
            pltpu.VMEM((groups, bands, own_in, positions), bf16),
            pltpu.VMEM((bands, own_in, positions), bf16),
            pltpu.VMEM((chips, all_frames, 9 * own_in, LANES), f32),
            pltpu.VMEM((frames, own_in, plane), f32),
            pltpu.VMEM((frames, own_in, plane), f32),
            pltpu.VMEM((bands, own_in, positions), f32),
            pltpu.VMEM((bands, own_in, positions), f32),
            pltpu.VMEM((all_frames, 9 * own_in, plane), bf16),
            dma((3,)),
            dma((4,)),
            dma((chips // 2, groups)),
            dma((chips // 2, groups)),
            dma((2, chips // 2, groups)),
            dma,
            dma,
            dma,
            dma,
            dma,
            dma,
            dma,
            dma,
            dma((frames,)),
            dma((frames,)),
            dma,
            dma,
        ],
        compiler_params=pltpu.CompilerParams(
            collective_id=0, has_side_effects=True, vmem_limit_bytes=64 * 2**20
        ),
    )(inputs, cotangent, kernel)


def local(inputs, cotangent, kernel):
    if exchange_fits(inputs, cotangent, kernel):
        return exchange_plan(inputs, cotangent, kernel)
    return gathered_plan(inputs, cotangent, kernel)


def solution(mesh):
    return jax.shard_map(
        local,
        mesh=mesh,
        in_specs=(P("tm", "rows", None, None), P("tm", "rows", None, None), P(None, "rows", "tm")),
        out_specs=(P("tm", "rows", None, None), P(None, "rows", "tm")),
        check_vma=False,
    )
```

```python
import functools

import jax
import jax.numpy as jnp
from jax import lax
from jax.experimental import pallas as pl
from jax.experimental.pallas import tpu as pltpu
from jax.sharding import PartitionSpec as P

MESH = pl.DeviceIdType.MESH
LANES = 128


def extended(block, sides, width):
    for axis, dim in sides:
        count = lax.axis_size(axis)
        forward = [(i, i + 1) for i in range(count - 1)]
        backward = [(target, source) for source, target in forward]
        low = lax.ppermute(
            lax.slice_in_dim(block, block.shape[dim] - width, None, axis=dim), axis, forward
        )
        high = lax.ppermute(lax.slice_in_dim(block, 0, width, axis=dim), axis, backward)
        block = jnp.concatenate([low, block, high], axis=dim)
    return block


def silu_slope(values):
    logistic = jax.nn.sigmoid(values)
    return logistic * (1.0 + values * (1.0 - logistic))


def widen_cols(values):
    return jnp.pad(values, ((0, 0), (0, 0), (1, 1), (0, 0)))


def tap_columns(padded, frames, height, across):
    pieces = []
    for time_tap in range(3):
        for row_tap in range(3):
            for col_tap in range(3):
                start_time, start_row, start_col = (2 - time_tap, 2 - row_tap, 2 - col_tap)
                pieces.append(
                    padded[
                        start_time : start_time + frames,
                        start_row : start_row + height,
                        start_col : start_col + across,
                    ]
                )
    stacked = jnp.stack(pieces, 3)
    return stacked.reshape(frames * height * across, 27, padded.shape[3])


def backward_piece(columns, portion):
    return lax.dot_general(
        columns, portion, (((1, 2), (0, 2)), ((), ())), preferred_element_type=jnp.float32
    )


def kernel_grad(haloed, gradient, factor):
    height = gradient.shape[1]
    across = gradient.shape[2]
    channels = haloed.shape[3]
    split_grads = lax.all_to_all(gradient, "tm", split_axis=3, concat_axis=0, tiled=True)
    width_out = split_grads.shape[3]
    padded_grads = jnp.pad(split_grads, ((0, 2), (0, 0), (0, 0), (0, 0)))
    portion = lax.all_gather(haloed, "tm", axis=0, tiled=True)
    offset = jnp.int32(0)
    portion_frames = portion.shape[0]
    widened = widen_cols(portion)
    spatial = jnp.stack(
        [
            widened[:, row_tap : row_tap + height, col_tap : col_tap + across]
            for row_tap in range(3)
            for col_tap in range(3)
        ],
        3,
    )
    shifted_grads = jnp.stack(
        [
            lax.dynamic_slice_in_dim(padded_grads, offset + 2 - time_tap, portion_frames, 0)
            for time_tap in range(3)
        ],
        0,
    )
    contribution = lax.dot_general(
        spatial,
        shifted_grads,
        (((0, 1, 2), (1, 2, 3)), ((), ())),
        preferred_element_type=jnp.float32,
    )
    contribution = jnp.transpose(contribution, (2, 0, 1, 3)).reshape(27, channels, width_out)
    return lax.psum_scatter(contribution * factor, "rows", scatter_dimension=1, tiled=True)


def gathered_plan(inputs, cotangent, kernel):
    frames, height, across, channels = inputs.shape
    positions = frames * height * across
    rows_kernel = lax.all_gather(kernel, "rows", axis=1, tiled=True)
    act = jax.nn.silu(inputs.astype(jnp.float32)).astype(jnp.bfloat16)
    paired = jnp.concatenate([act, cotangent], 3)
    paired_rows = extended(paired, (("rows", 1),), 1)
    halo_act = paired_rows[:, :, :, :channels]
    halo_grad = paired_rows[:, :, :, channels:]
    split_bands = lax.all_to_all(halo_grad, "tm", split_axis=3, concat_axis=0, tiled=True)
    total_frames = split_bands.shape[0]
    padded_bands = jnp.pad(split_bands, ((0, 2), (0, 0), (0, 0), (0, 0)))
    cols_all = tap_columns(widen_cols(padded_bands), total_frames, height, across)
    partial_terms = backward_piece(cols_all, rows_kernel).reshape(
        total_frames // frames, positions, channels
    )
    grad_act = lax.psum_scatter(partial_terms, "tm", scatter_dimension=0, tiled=True)
    grad_act = grad_act.reshape(frames, height, across, channels)
    grad_inputs = (
        cotangent.astype(jnp.float32) + grad_act * silu_slope(inputs.astype(jnp.float32))
    ).astype(jnp.bfloat16)
    factor = float(frames * lax.axis_size("tm") * height * lax.axis_size("rows") * across) ** (-0.5)
    grad_kernel = kernel_grad(halo_act, cotangent, factor)
    return (grad_inputs, grad_kernel)


def exchange_fits(inputs, cotangent, kernel):
    frames, height, across, channels = inputs.shape
    groups, bands = lax.axis_size("tm"), lax.axis_size("rows")
    own_in, own_out = kernel.shape[1], kernel.shape[2]
    return (
        frames == 2
        and frames * height * across == LANES
        and across == 16
        and own_in == 16
        and own_out == LANES
        and groups == 2
        and bands == 16
        and channels == own_in * bands == own_out * groups
        and frames * groups * height * bands * across * own_out * 2 <= 4 * 2**20
    )


def exchange_kernel(
    groups, bands, factor,
    inputs_hbm, cot_hbm, kernel_hbm, grad_in_hbm, grad_kernel_hbm,
    inputs_ref, cot_ref, kernel_ref, grad_in_ref, grad_kernel_ref, grads, acts, act_send, sums, part_send, part, back_send, back,
    spatial, load_sem, store_sem, line_recv, side_recv, core_recv, line_send, side_send, core_send, own_sem,
    act_send_sem, act_recv_sem, cross_send_sem, cross_recv_sem, part_send_sem, part_recv_sem,
    back_send_sem, back_recv_sem,
):
    frames, height, across, channels = inputs_ref.shape
    own_in = kernel_ref.shape[1]
    positions = frames * height * across
    rows = height * bands
    plane = rows * across
    all_frames = frames * groups
    chips = bands // 2
    depth = chips // 2
    half = LANES // 2

    group, band = lax.axis_index("tm"), lax.axis_index("rows")
    partner = (group + 1) % groups
    chip, core = band // 2, band % 2
    layer, column = chip // 2, chip % 2

    def layer_at(turn):
        return (layer // 2 + turn // 2) % 2 * 2 + (layer + turn) % 2

    def chip_at(layer_of, column_of):
        return layer_of * 2 + column_of

    def region(group_of, band_of):
        return grads.at[pl.ds(group_of * frames, frames), pl.ds(band_of * height, height)]

    def wait_bytes(ref, sem):
        pltpu.make_async_copy(ref, ref, sem).wait()

    barrier = pltpu.get_barrier_semaphore()

    def greet(step, carry):
        pl.semaphore_signal(
            barrier, inc=1, device_id=(group, (band + step) % bands), device_id_type=MESH
        )
        return carry

    lax.fori_loop(1, bands, greet, 0)
    for layer_of in range(depth):
        pl.semaphore_signal(
            barrier, inc=1, device_id=(partner, chip_at(layer_of, column) * 2 + core),
            device_id_type=MESH,
        )

    load_inputs = pltpu.make_async_copy(inputs_hbm, inputs_ref, load_sem.at[0])
    load_cot = pltpu.make_async_copy(cot_hbm, cot_ref, load_sem.at[1])
    load_kernel = pltpu.make_async_copy(kernel_hbm, kernel_ref, load_sem.at[2])
    load_inputs.start()
    load_cot.start()
    load_kernel.start()

    load_cot.wait()
    own_part = cot_ref.at[:, :, :, pl.ds(pl.multiple_of(group * LANES, LANES), LANES)]
    other_part = cot_ref.at[:, :, :, pl.ds(pl.multiple_of(partner * LANES, LANES), LANES)]
    own_copy = pltpu.make_async_copy(own_part, region(group, band), own_sem)
    own_copy.start()
    load_inputs.wait()
    values = inputs_ref[...].reshape(positions, channels).astype(jnp.float32)
    act = values * jax.nn.sigmoid(values)
    act_send[...] = act.T.astype(jnp.bfloat16).reshape(bands, own_in, positions)
    own_copy.wait()
    pl.semaphore_wait(barrier, bands - 1 + depth)

    def send_line(source, piece, layer_of):
        pltpu.make_async_remote_copy(
            src_ref=source, dst_ref=region(group, band),
            send_sem=line_send, recv_sem=line_recv.at[layer, piece],
            device_id=((group + piece) % groups, chip_at(layer_of, column) * 2 + core),
            device_id_type=MESH,
        ).start()

    def to_other_column(source, piece, layer_of):
        pltpu.make_async_remote_copy(
            src_ref=source,
            dst_ref=region((group + piece) % groups, chip_at(layer_of, column) * 2 + core),
            send_sem=side_send, recv_sem=side_recv.at[layer_of, piece],
            device_id=(group, chip_at(layer, 1 - column) * 2 + core), device_id_type=MESH,
        ).start()

    def to_other_core(source, piece, layer_of, side):
        column_of = column + side - 2 * column * side
        pltpu.make_async_remote_copy(
            src_ref=source,
            dst_ref=region((group + piece) % groups, chip_at(layer_of, column_of) * 2 + core),
            send_sem=core_send, recv_sem=core_recv.at[side, layer_of, piece],
            device_id=(group, chip * 2 + 1 - core), device_id_type=MESH,
        ).start()

    def send_act(step, carry):
        target = (band + step) % bands
        pltpu.make_async_remote_copy(
            src_ref=act_send.at[target], dst_ref=acts.at[group, band],
            send_sem=act_send_sem, recv_sem=act_recv_sem,
            device_id=(group, target), device_id_type=MESH,
        ).start()
        return carry

    send_line(other_part, 1, layer)

    def send_lines(turn, carry):
        send_line(own_part, 0, layer_at(turn))
        send_line(other_part, 1, layer_at(turn))
        return carry

    lax.fori_loop(1, depth, send_lines, 0)
    own_act = pltpu.make_async_copy(act_send.at[band], acts.at[group, band], act_recv_sem)
    own_act.start()

    def pass_line(turn):
        layer_of = layer_at(turn)
        for piece in range(groups):
            arrived = region((group + piece) % groups, chip_at(layer_of, column) * 2 + core)
            if piece:
                wait_bytes(arrived, line_recv.at[layer_of, piece])
            else:
                pl.when(turn > 0)(
                    functools.partial(wait_bytes, arrived, line_recv.at[layer_of, piece])
                )
            to_other_column(arrived, piece, layer_of)
            to_other_core(arrived, piece, layer_of, 0)

    def pass_side(turn):
        for piece in range(groups):
            layer_of = layer_at(turn)
            arrived = region((group + piece) % groups, chip_at(layer_of, 1 - column) * 2 + core)
            wait_bytes(arrived, side_recv.at[layer_of, piece])
            to_other_core(arrived, piece, layer_of, 1)

    lane = lax.broadcasted_iota(jnp.int32, (own_in, plane), 1)
    col, row = lane % across, lane // across
    low = lax.broadcasted_iota(jnp.int32, (own_in, LANES), 1) < half

    def moved(block, by_row, by_col):
        shift = by_row * across + by_col
        if shift == 0:
            return block
        block = pltpu.roll(block, (-shift) % plane, 1)
        inside = None
        if by_row:
            inside = (row + by_row >= 0) & (row + by_row < rows)
        if by_col:
            in_cols = (col + by_col >= 0) & (col + by_col < across)
            inside = in_cols if inside is None else inside & in_cols
        return jnp.where(inside, block, 0.0)

    def sum_taps(chip_of):
        taps = jnp.concatenate(
            [kernel_ref[pl.ds(9 * tap, 9)].reshape(9 * own_in, LANES) for tap in range(3)], axis=1
        )
        cells = [
            grads[frame, pl.ds(chip_of * 2 * height, 2 * height)].reshape(LANES, LANES)
            for frame in range(all_frames)
        ]
        for frame in range(all_frames):
            first = max(0, frame + 3 - all_frames)
            window = jnp.concatenate(
                [cells[frame + 2 - tap] for tap in range(first, 3)], axis=1
            )
            sums[chip_of, frame] = lax.dot_general(
                taps[:, first * LANES :], window, (((1,), (1,)), ((), ())),
                preferred_element_type=jnp.float32,
            )

    def sum_chip(turn, side):
        layer_of = layer_at(turn)
        chip_of = chip_at(layer_of, column + side - 2 * column * side)
        for piece in range(groups):
            arrived = region((group + piece) % groups, chip_of * 2 + 1 - core)
            wait_bytes(arrived, core_recv.at[side, layer_of, piece])
        sum_taps(chip_of)

    def shift_acts(group_of, carry):
        for at in range(frames):
            tiles = []
            for pair in range(bands // 2):
                x = acts[group_of, 2 * pair].astype(jnp.float32)
                y = acts[group_of, 2 * pair + 1].astype(jnp.float32)
                if at == 0:
                    tiles.append(jnp.where(low, x, pltpu.roll(y, half, 1)))
                else:
                    tiles.append(jnp.where(low, pltpu.roll(x, half, 1), y))
            whole = jnp.concatenate(tiles, axis=1)
            for col_tap in range(3):
                shifted = moved(whole, 0, col_tap - 1)
                for row_tap in range(3):
                    tap = 3 * row_tap + col_tap
                    spatial[2 + group_of * frames + at, pl.ds(tap * own_in, own_in)] = moved(
                        shifted, row_tap - 1, 0
                    ).astype(jnp.bfloat16)
        return carry

    load_kernel.wait()
    spatial[pl.ds(0, 2)] = jnp.zeros((2,) + spatial.shape[1:], spatial.dtype)

    def turns(turn, carry):
        @pl.when(turn < depth)
        def _():
            pass_line(turn)

        @pl.when((turn >= 1) & (turn <= depth))
        def _():
            pass_side(turn - 1)

        @pl.when(turn == 0)
        def _():
            lax.fori_loop(1, bands, send_act, 0)

        @pl.when(turn == 2)
        def _():
            wait_bytes(acts.at[group], act_recv_sem)
            pltpu.make_async_remote_copy(
                src_ref=acts.at[group], dst_ref=acts.at[group],
                send_sem=cross_send_sem, recv_sem=cross_recv_sem,
                device_id=(partner, band), device_id_type=MESH,
            ).start()

        def sides(side, carry):
            at = turn - 1 - side

            @pl.when((at >= 0) & (at < depth))
            def _():
                sum_chip(at, side)

            return carry

        return lax.fori_loop(0, 2, sides, carry)

    lax.fori_loop(0, depth + 2, turns, 0)

    def grad_act_of(frame):
        result = None
        for col_tap in range(3):
            mixed = None
            for row_tap in range(3):
                tap = 3 * row_tap + col_tap
                term = jnp.concatenate(
                    [sums[at, frame, pl.ds(tap * own_in, own_in)] for at in range(chips)], axis=1
                )
                term = moved(term, 1 - row_tap, 0)
                mixed = term if mixed is None else mixed + term
            mixed = moved(mixed, 0, 1 - col_tap)
            result = mixed if result is None else result + mixed
        return result

    def shares(at, carry):
        owner = (partner + at // frames) % groups
        part_send[at] = grad_act_of(owner * frames + at % frames)

        @pl.when(at < frames)
        def _():
            pltpu.make_async_remote_copy(
                src_ref=part_send.at[at], dst_ref=part.at[at],
                send_sem=part_send_sem.at[at], recv_sem=part_recv_sem.at[at],
                device_id=(partner, band), device_id_type=MESH,
            ).start()

        return carry

    lax.fori_loop(0, all_frames, shares, 0)

    wait_bytes(acts.at[partner], cross_recv_sem)
    lax.fori_loop(0, groups, shift_acts, 0)

    grad_kernel_ref[...] = jnp.zeros_like(grad_kernel_ref)

    def kernel_taps(frame, carry):
        cells = grads[frame].reshape(plane, LANES)
        for time_tap in range(3):
            term = lax.dot_general(
                spatial[frame + time_tap], cells, (((1,), (0,)), ((), ())),
                preferred_element_type=jnp.float32,
            )
            own = pl.ds(9 * time_tap, 9)
            grad_kernel_ref[own] = grad_kernel_ref[own] + term.reshape(9, own_in, LANES)
        return carry

    for at in range(frames):
        wait_bytes(part.at[at], part_recv_sem.at[at])
    first, second = [part_send[frames + at] + part[at] for at in range(frames)]
    for pair in range(bands // 2):
        x = first[:, pair * LANES : (pair + 1) * LANES]
        y = second[:, pair * LANES : (pair + 1) * LANES]
        back_send[2 * pair] = jnp.where(low, x, pltpu.roll(y, half, 1))
        back_send[2 * pair + 1] = jnp.where(low, pltpu.roll(x, half, 1), y)

    def send_back(step, carry):
        target = (band + step) % bands
        pltpu.make_async_remote_copy(
            src_ref=back_send.at[target], dst_ref=back.at[band],
            send_sem=back_send_sem, recv_sem=back_recv_sem,
            device_id=(group, target), device_id_type=MESH,
        ).start()
        return carry

    lax.fori_loop(1, bands, send_back, 0)
    own_back = pltpu.make_async_copy(back_send.at[band], back.at[band], back_recv_sem)
    own_back.start()

    lax.fori_loop(0, all_frames, kernel_taps, 0)
    grad_kernel_ref[...] = grad_kernel_ref[...] * factor
    store_kernel = pltpu.make_async_copy(grad_kernel_ref, grad_kernel_hbm, store_sem.at[0])
    store_kernel.start()

    wait_bytes(back, back_recv_sem)
    grad_act = back[...].reshape(channels, positions).T
    values = inputs_ref[...].reshape(positions, channels).astype(jnp.float32)
    cot = cot_ref[...].reshape(positions, channels).astype(jnp.float32)
    grad_in = cot + grad_act * silu_slope(values)
    grad_in_ref[...] = grad_in.astype(jnp.bfloat16).reshape(grad_in_ref.shape)
    store_in = pltpu.make_async_copy(grad_in_ref, grad_in_hbm, store_sem.at[1])
    store_in.start()

    line_rows = height * (2 * depth - 1)
    wait_bytes(grads.at[pl.ds(0, frames), pl.ds(0, line_rows)], line_send)
    wait_bytes(grads.at[pl.ds(0, frames), pl.ds(0, rows // 2)], side_send)
    wait_bytes(grads.at[:, pl.ds(0, rows // 2)], core_send)
    wait_bytes(acts.at[0, pl.ds(0, bands - 1)], act_send_sem)
    wait_bytes(acts.at[group], cross_send_sem)
    for at in range(frames):
        wait_bytes(part_send.at[at], part_send_sem.at[at])
    wait_bytes(back.at[pl.ds(0, bands - 1)], back_send_sem)
    store_kernel.wait()
    store_in.wait()


def exchange_plan(inputs, cotangent, kernel):
    frames, height, across, channels = inputs.shape
    taps, own_in, own_out = kernel.shape
    groups, bands = lax.axis_size("tm"), lax.axis_size("rows")
    positions = frames * height * across
    all_frames, rows = frames * groups, height * bands
    chips, plane = bands // 2, rows * across
    factor = float(all_frames * plane) ** (-0.5)
    dma = pltpu.SemaphoreType.DMA
    bf16, f32 = jnp.bfloat16, jnp.float32
    return pl.pallas_call(
        functools.partial(exchange_kernel, groups, bands, factor),
        out_shape=(
            jax.ShapeDtypeStruct(inputs.shape, bf16),
            jax.ShapeDtypeStruct(kernel.shape, f32),
        ),
        in_specs=[pl.BlockSpec(memory_space=pltpu.HBM)] * 3,
        out_specs=[pl.BlockSpec(memory_space=pltpu.HBM)] * 2,
        scratch_shapes=[
            pltpu.VMEM(inputs.shape, bf16),
            pltpu.VMEM(cotangent.shape, bf16),
            pltpu.VMEM(kernel.shape, bf16),
            pltpu.VMEM(inputs.shape, bf16),
            pltpu.VMEM(kernel.shape, f32),
            pltpu.VMEM((all_frames, rows, across, own_out), bf16),
            pltpu.VMEM((groups, bands, own_in, positions), bf16),
            pltpu.VMEM((bands, own_in, positions), bf16),
            pltpu.VMEM((chips, all_frames, 9 * own_in, LANES), f32),
            pltpu.VMEM((all_frames, own_in, plane), f32),
            pltpu.VMEM((frames, own_in, plane), f32),
            pltpu.VMEM((bands, own_in, positions), f32),
            pltpu.VMEM((bands, own_in, positions), f32),
            pltpu.VMEM((all_frames + 2, 9 * own_in, plane), bf16),
            dma((3,)),
            dma((2,)),
            dma((chips // 2, groups)),
            dma((chips // 2, groups)),
            dma((2, chips // 2, groups)),
            dma,
            dma,
            dma,
            dma,
            dma,
            dma,
            dma,
            dma,
            dma((frames,)),
            dma((frames,)),
            dma,
            dma,
        ],
        compiler_params=pltpu.CompilerParams(
            collective_id=0, has_side_effects=True, vmem_limit_bytes=64 * 2**20
        ),
    )(inputs, cotangent, kernel)


def local(inputs, cotangent, kernel):
    if exchange_fits(inputs, cotangent, kernel):
        return exchange_plan(inputs, cotangent, kernel)
    return gathered_plan(inputs, cotangent, kernel)


def solution(mesh):
    return jax.shard_map(
        local,
        mesh=mesh,
        in_specs=(P("tm", "rows", None, None), P("tm", "rows", None, None), P(None, "rows", "tm")),
        out_specs=(P("tm", "rows", None, None), P(None, "rows", "tm")),
        check_vma=False,
    )
```

```python
import functools

import jax
import jax.numpy as jnp
from jax import lax
from jax.experimental import pallas as pl
from jax.experimental.pallas import tpu as pltpu
from jax.sharding import PartitionSpec as P

MESH = pl.DeviceIdType.MESH
LANES = 128


def extended(block, sides, width):
    for axis, dim in sides:
        count = lax.axis_size(axis)
        forward = [(i, i + 1) for i in range(count - 1)]
        backward = [(target, source) for source, target in forward]
        low = lax.ppermute(
            lax.slice_in_dim(block, block.shape[dim] - width, None, axis=dim), axis, forward
        )
        high = lax.ppermute(lax.slice_in_dim(block, 0, width, axis=dim), axis, backward)
        block = jnp.concatenate([low, block, high], axis=dim)
    return block


def silu_slope(values):
    logistic = jax.nn.sigmoid(values)
    return logistic * (1.0 + values * (1.0 - logistic))


def widen_cols(values):
    return jnp.pad(values, ((0, 0), (0, 0), (1, 1), (0, 0)))


def tap_columns(padded, frames, height, across):
    pieces = []
    for time_tap in range(3):
        for row_tap in range(3):
            for col_tap in range(3):
                start_time, start_row, start_col = (2 - time_tap, 2 - row_tap, 2 - col_tap)
                pieces.append(
                    padded[
                        start_time : start_time + frames,
                        start_row : start_row + height,
                        start_col : start_col + across,
                    ]
                )
    stacked = jnp.stack(pieces, 3)
    return stacked.reshape(frames * height * across, 27, padded.shape[3])


def backward_piece(columns, portion):
    return lax.dot_general(
        columns, portion, (((1, 2), (0, 2)), ((), ())), preferred_element_type=jnp.float32
    )


def kernel_grad(haloed, gradient, factor):
    height = gradient.shape[1]
    across = gradient.shape[2]
    channels = haloed.shape[3]
    split_grads = lax.all_to_all(gradient, "tm", split_axis=3, concat_axis=0, tiled=True)
    width_out = split_grads.shape[3]
    padded_grads = jnp.pad(split_grads, ((0, 2), (0, 0), (0, 0), (0, 0)))
    portion = lax.all_gather(haloed, "tm", axis=0, tiled=True)
    offset = jnp.int32(0)
    portion_frames = portion.shape[0]
    widened = widen_cols(portion)
    spatial = jnp.stack(
        [
            widened[:, row_tap : row_tap + height, col_tap : col_tap + across]
            for row_tap in range(3)
            for col_tap in range(3)
        ],
        3,
    )
    shifted_grads = jnp.stack(
        [
            lax.dynamic_slice_in_dim(padded_grads, offset + 2 - time_tap, portion_frames, 0)
            for time_tap in range(3)
        ],
        0,
    )
    contribution = lax.dot_general(
        spatial,
        shifted_grads,
        (((0, 1, 2), (1, 2, 3)), ((), ())),
        preferred_element_type=jnp.float32,
    )
    contribution = jnp.transpose(contribution, (2, 0, 1, 3)).reshape(27, channels, width_out)
    return lax.psum_scatter(contribution * factor, "rows", scatter_dimension=1, tiled=True)


def gathered_plan(inputs, cotangent, kernel):
    frames, height, across, channels = inputs.shape
    positions = frames * height * across
    rows_kernel = lax.all_gather(kernel, "rows", axis=1, tiled=True)
    act = jax.nn.silu(inputs.astype(jnp.float32)).astype(jnp.bfloat16)
    paired = jnp.concatenate([act, cotangent], 3)
    paired_rows = extended(paired, (("rows", 1),), 1)
    halo_act = paired_rows[:, :, :, :channels]
    halo_grad = paired_rows[:, :, :, channels:]
    split_bands = lax.all_to_all(halo_grad, "tm", split_axis=3, concat_axis=0, tiled=True)
    total_frames = split_bands.shape[0]
    padded_bands = jnp.pad(split_bands, ((0, 2), (0, 0), (0, 0), (0, 0)))
    cols_all = tap_columns(widen_cols(padded_bands), total_frames, height, across)
    partial_terms = backward_piece(cols_all, rows_kernel).reshape(
        total_frames // frames, positions, channels
    )
    grad_act = lax.psum_scatter(partial_terms, "tm", scatter_dimension=0, tiled=True)
    grad_act = grad_act.reshape(frames, height, across, channels)
    grad_inputs = (
        cotangent.astype(jnp.float32) + grad_act * silu_slope(inputs.astype(jnp.float32))
    ).astype(jnp.bfloat16)
    factor = float(frames * lax.axis_size("tm") * height * lax.axis_size("rows") * across) ** (-0.5)
    grad_kernel = kernel_grad(halo_act, cotangent, factor)
    return (grad_inputs, grad_kernel)


def exchange_fits(inputs, cotangent, kernel):
    frames, height, across, channels = inputs.shape
    groups, bands = lax.axis_size("tm"), lax.axis_size("rows")
    own_in, own_out = kernel.shape[1], kernel.shape[2]
    return (
        frames == 2
        and frames * height * across == LANES
        and across == 16
        and own_in == 16
        and own_out == LANES
        and groups == 2
        and bands == 16
        and channels == own_in * bands == own_out * groups
        and frames * groups * height * bands * across * own_out * 2 <= 4 * 2**20
    )


def exchange_kernel(
    groups, bands, factor,
    inputs_hbm, cot_hbm, kernel_hbm, grad_in_ref, grad_kernel_ref,
    inputs_ref, cot_ref, kernel_ref, turned, grads, acts, act_send, sums, part_send, part, back_send, back,
    spatial, load_sem, line_recv, side_recv, core_recv, line_send, side_send, core_send, own_sem,
    act_send_sem, act_recv_sem, cross_send_sem, cross_recv_sem, part_send_sem, part_recv_sem,
    back_send_sem, back_recv_sem,
):
    frames, height, across, channels = inputs_ref.shape
    own_in = kernel_ref.shape[1]
    positions = frames * height * across
    rows = height * bands
    plane = rows * across
    all_frames = frames * groups
    chips = bands // 2
    depth = chips // 2
    half = LANES // 2

    group, band = lax.axis_index("tm"), lax.axis_index("rows")
    partner = (group + 1) % groups
    chip, core = band // 2, band % 2
    layer, column = chip // 2, chip % 2

    def layer_at(turn):
        return (layer // 2 + turn // 2) % 2 * 2 + (layer + turn) % 2

    def chip_at(layer_of, column_of):
        return layer_of * 2 + column_of

    def region(group_of, band_of):
        return grads.at[pl.ds(group_of * frames, frames), pl.ds(band_of * height, height)]

    def wait_bytes(ref, sem):
        pltpu.make_async_copy(ref, ref, sem).wait()

    load_inputs = pltpu.make_async_copy(inputs_hbm, inputs_ref, load_sem.at[0])
    load_cot = pltpu.make_async_copy(cot_hbm, cot_ref, load_sem.at[1])
    load_kernel = pltpu.make_async_copy(kernel_hbm, kernel_ref, load_sem.at[2])
    load_inputs.start()
    load_cot.start()
    load_kernel.start()

    barrier = pltpu.get_barrier_semaphore()

    def greet(step, carry):
        pl.semaphore_signal(
            barrier, inc=1, device_id=(group, (band + step) % bands), device_id_type=MESH
        )
        return carry

    lax.fori_loop(1, bands, greet, 0)
    for layer_of in range(depth):
        pl.semaphore_signal(
            barrier, inc=1, device_id=(partner, chip_at(layer_of, column) * 2 + core),
            device_id_type=MESH,
        )

    own_part = cot_hbm.at[:, :, :, pl.ds(pl.multiple_of(group * LANES, LANES), LANES)]
    other_part = cot_hbm.at[:, :, :, pl.ds(pl.multiple_of(partner * LANES, LANES), LANES)]
    own_copy = pltpu.make_async_copy(own_part, region(group, band), own_sem)
    own_copy.start()
    pl.semaphore_wait(barrier, bands - 1 + depth)

    def send_line(source, piece, layer_of):
        pltpu.make_async_remote_copy(
            src_ref=source, dst_ref=region(group, band),
            send_sem=line_send, recv_sem=line_recv.at[layer, piece],
            device_id=((group + piece) % groups, chip_at(layer_of, column) * 2 + core),
            device_id_type=MESH,
        ).start()

    def to_other_column(source, piece, layer_of):
        pltpu.make_async_remote_copy(
            src_ref=source,
            dst_ref=region((group + piece) % groups, chip_at(layer_of, column) * 2 + core),
            send_sem=side_send, recv_sem=side_recv.at[layer_of, piece],
            device_id=(group, chip_at(layer, 1 - column) * 2 + core), device_id_type=MESH,
        ).start()

    def to_other_core(source, piece, layer_of, side):
        column_of = column + side - 2 * column * side
        pltpu.make_async_remote_copy(
            src_ref=source,
            dst_ref=region((group + piece) % groups, chip_at(layer_of, column_of) * 2 + core),
            send_sem=core_send, recv_sem=core_recv.at[side, layer_of, piece],
            device_id=(group, chip * 2 + 1 - core), device_id_type=MESH,
        ).start()

    def send_act(step, carry):
        target = (band + step) % bands
        pltpu.make_async_remote_copy(
            src_ref=act_send.at[target], dst_ref=acts.at[group, band],
            send_sem=act_send_sem, recv_sem=act_recv_sem,
            device_id=(group, target), device_id_type=MESH,
        ).start()
        return carry

    send_line(other_part, 1, layer)

    def send_lines(turn, carry):
        send_line(own_part, 0, layer_at(turn))
        send_line(other_part, 1, layer_at(turn))
        return carry

    lax.fori_loop(1, depth, send_lines, 0)
    load_inputs.wait()
    values = inputs_ref[...].reshape(positions, channels).astype(jnp.float32)
    act = values * jax.nn.sigmoid(values)
    act_send[...] = act.T.astype(jnp.bfloat16).reshape(bands, own_in, positions)
    own_copy.wait()
    own_act = pltpu.make_async_copy(act_send.at[band], acts.at[group, band], act_recv_sem)
    own_act.start()

    def pass_line(turn):
        layer_of = layer_at(turn)
        for piece in range(groups):
            arrived = region((group + piece) % groups, chip_at(layer_of, column) * 2 + core)
            if piece:
                wait_bytes(arrived, line_recv.at[layer_of, piece])
            else:
                pl.when(turn > 0)(
                    functools.partial(wait_bytes, arrived, line_recv.at[layer_of, piece])
                )
            to_other_column(arrived, piece, layer_of)
            to_other_core(arrived, piece, layer_of, 0)

    def pass_side(turn):
        for piece in range(groups):
            layer_of = layer_at(turn)
            arrived = region((group + piece) % groups, chip_at(layer_of, 1 - column) * 2 + core)
            wait_bytes(arrived, side_recv.at[layer_of, piece])
            to_other_core(arrived, piece, layer_of, 1)

    lane = lax.broadcasted_iota(jnp.int32, (own_in, plane), 1)
    col, row = lane % across, lane // across
    low = lax.broadcasted_iota(jnp.int32, (own_in, LANES), 1) < half

    def moved(block, by_row, by_col):
        shift = by_row * across + by_col
        if shift == 0:
            return block
        block = pltpu.roll(block, (-shift) % plane, 1)
        inside = None
        if by_row:
            inside = (row + by_row >= 0) & (row + by_row < rows)
        if by_col:
            in_cols = (col + by_col >= 0) & (col + by_col < across)
            inside = in_cols if inside is None else inside & in_cols
        return jnp.where(inside, block, 0.0)

    def turn_kernel():
        for time_tap in range(3):
            for row_tap in range(3):
                block = kernel_ref[pl.ds(9 * time_tap + 3 * row_tap, 3)]
                block = block.reshape(3 * own_in, LANES).astype(jnp.float32)
                block = jnp.concatenate(
                    [block, jnp.zeros((LANES - 3 * own_in, LANES), jnp.float32)], axis=0
                )
                turned[pl.ds(time_tap * LANES, LANES), pl.ds(row_tap * LANES, LANES)] = (
                    block.T.astype(jnp.bfloat16)
                )

    def sum_taps(chip_of):
        cells = [
            grads[frame, pl.ds(chip_of * 2 * height, 2 * height)].reshape(LANES, LANES)
            for frame in range(all_frames)
        ] + [jnp.zeros((LANES, LANES), jnp.bfloat16)] * 2
        windows = jnp.concatenate(
            [
                jnp.concatenate([cells[frame + 2 - tap] for tap in range(3)], axis=1)
                for frame in range(all_frames)
            ],
            axis=0,
        )
        result = lax.dot_general(
            windows, turned[...], (((1,), (0,)), ((), ())), preferred_element_type=jnp.float32
        )
        place = pl.ds(pl.multiple_of(across + chip_of * LANES, across), LANES)
        for row_tap in range(3):
            for frame in range(all_frames):
                sums[row_tap, frame, place] = result[
                    frame * LANES : (frame + 1) * LANES, row_tap * LANES : (row_tap + 1) * LANES
                ]

    def sum_chip(turn, side):
        layer_of = layer_at(turn)
        chip_of = chip_at(layer_of, column + side - 2 * column * side)
        for piece in range(groups):
            arrived = region((group + piece) % groups, chip_of * 2 + 1 - core)
            wait_bytes(arrived, core_recv.at[side, layer_of, piece])
        sum_taps(chip_of)

    def shift_acts(group_of, carry):
        for at in range(frames):
            tiles = []
            for pair in range(bands // 2):
                x = acts[group_of, 2 * pair].astype(jnp.float32)
                y = acts[group_of, 2 * pair + 1].astype(jnp.float32)
                if at == 0:
                    tiles.append(jnp.where(low, x, pltpu.roll(y, half, 1)))
                else:
                    tiles.append(jnp.where(low, pltpu.roll(x, half, 1), y))
            whole = jnp.concatenate(tiles, axis=1)
            for col_tap in range(3):
                shifted = moved(whole, 0, col_tap - 1)
                for row_tap in range(3):
                    tap = 3 * row_tap + col_tap
                    spatial[2 + group_of * frames + at, pl.ds(tap * own_in, own_in)] = moved(
                        shifted, row_tap - 1, 0
                    ).astype(jnp.bfloat16)
        return carry

    load_kernel.wait()
    turn_kernel()
    sums[:, :, pl.ds(0, across)] = jnp.zeros((3, all_frames, across, LANES), jnp.float32)
    sums[:, :, pl.ds(across + plane, across)] = jnp.zeros((3, all_frames, across, LANES), jnp.float32)
    spatial[pl.ds(0, 2)] = jnp.zeros((2,) + spatial.shape[1:], spatial.dtype)

    def turns(turn, carry):
        @pl.when(turn < depth)
        def _():
            pass_line(turn)

        @pl.when((turn >= 1) & (turn <= depth))
        def _():
            pass_side(turn - 1)

        @pl.when(turn == 0)
        def _():
            lax.fori_loop(1, bands, send_act, 0)

        @pl.when(turn == 2)
        def _():
            wait_bytes(acts.at[group], act_recv_sem)
            pltpu.make_async_remote_copy(
                src_ref=acts.at[group], dst_ref=acts.at[group],
                send_sem=cross_send_sem, recv_sem=cross_recv_sem,
                device_id=(partner, band), device_id_type=MESH,
            ).start()

        def sides(side, carry):
            at = turn - 1 - side

            @pl.when((at >= 0) & (at < depth))
            def _():
                sum_chip(at, side)

            return carry

        return lax.fori_loop(0, 2, sides, carry)

    lax.fori_loop(0, depth + 2, turns, 0)

    def grad_act_of(frame):
        mixed = None
        for row_tap in range(3):
            term = sums[row_tap, frame, pl.ds(across * (2 - row_tap), plane)]
            mixed = term if mixed is None else mixed + term
        mixed = mixed.T
        result = None
        for col_tap in range(3):
            term = moved(mixed[col_tap * own_in : (col_tap + 1) * own_in], 0, 1 - col_tap)
            result = term if result is None else result + term
        return result

    def shares(at, carry):
        owner = (partner + at // frames) % groups
        part_send[at] = grad_act_of(owner * frames + at % frames)

        @pl.when(at < frames)
        def _():
            pltpu.make_async_remote_copy(
                src_ref=part_send.at[at], dst_ref=part.at[at],
                send_sem=part_send_sem.at[at], recv_sem=part_recv_sem.at[at],
                device_id=(partner, band), device_id_type=MESH,
            ).start()

        return carry

    lax.fori_loop(0, all_frames, shares, 0)

    wait_bytes(acts.at[partner], cross_recv_sem)
    lax.fori_loop(0, groups, shift_acts, 0)

    grad_kernel_ref[...] = jnp.zeros_like(grad_kernel_ref)

    def kernel_taps(frame, carry):
        cells = grads[frame].reshape(plane, LANES)
        for time_tap in range(3):
            term = lax.dot_general(
                spatial[frame + time_tap], cells, (((1,), (0,)), ((), ())),
                preferred_element_type=jnp.float32,
            )
            own = pl.ds(9 * time_tap, 9)
            grad_kernel_ref[own] = grad_kernel_ref[own] + term.reshape(9, own_in, LANES)
        return carry

    for at in range(frames):
        wait_bytes(part.at[at], part_recv_sem.at[at])
    first, second = [part_send[frames + at] + part[at] for at in range(frames)]
    for pair in range(bands // 2):
        x = first[:, pair * LANES : (pair + 1) * LANES]
        y = second[:, pair * LANES : (pair + 1) * LANES]
        back_send[2 * pair] = jnp.where(low, x, pltpu.roll(y, half, 1))
        back_send[2 * pair + 1] = jnp.where(low, pltpu.roll(x, half, 1), y)

    def send_back(step, carry):
        target = (band + step) % bands
        pltpu.make_async_remote_copy(
            src_ref=back_send.at[target], dst_ref=back.at[band],
            send_sem=back_send_sem, recv_sem=back_recv_sem,
            device_id=(group, target), device_id_type=MESH,
        ).start()
        return carry

    lax.fori_loop(1, bands, send_back, 0)
    own_back = pltpu.make_async_copy(back_send.at[band], back.at[band], back_recv_sem)
    own_back.start()

    lax.fori_loop(0, all_frames, kernel_taps, 0)
    grad_kernel_ref[...] = grad_kernel_ref[...] * factor

    wait_bytes(back, back_recv_sem)
    grad_act = back[...].reshape(channels, positions).T
    values = inputs_ref[...].reshape(positions, channels).astype(jnp.float32)
    load_cot.wait()
    cot = cot_ref[...].reshape(positions, channels).astype(jnp.float32)
    grad_in = cot + grad_act * silu_slope(values)
    grad_in_ref[...] = grad_in.astype(jnp.bfloat16).reshape(grad_in_ref.shape)

    line_rows = height * (2 * depth - 1)
    wait_bytes(grads.at[pl.ds(0, frames), pl.ds(0, line_rows)], line_send)
    wait_bytes(grads.at[pl.ds(0, frames), pl.ds(0, rows // 2)], side_send)
    wait_bytes(grads.at[:, pl.ds(0, rows // 2)], core_send)
    wait_bytes(acts.at[0, pl.ds(0, bands - 1)], act_send_sem)
    wait_bytes(acts.at[group], cross_send_sem)
    for at in range(frames):
        wait_bytes(part_send.at[at], part_send_sem.at[at])
    wait_bytes(back.at[pl.ds(0, bands - 1)], back_send_sem)


def exchange_plan(inputs, cotangent, kernel):
    frames, height, across, channels = inputs.shape
    taps, own_in, own_out = kernel.shape
    groups, bands = lax.axis_size("tm"), lax.axis_size("rows")
    positions = frames * height * across
    all_frames, rows = frames * groups, height * bands
    chips, plane = bands // 2, rows * across
    factor = float(all_frames * plane) ** (-0.5)
    dma = pltpu.SemaphoreType.DMA
    bf16, f32 = jnp.bfloat16, jnp.float32
    return pl.pallas_call(
        functools.partial(exchange_kernel, groups, bands, factor),
        out_shape=(
            pltpu.VMEM(inputs.shape, bf16),
            pltpu.VMEM(kernel.shape, f32),
        ),
        in_specs=[pl.BlockSpec(memory_space=pltpu.HBM)] * 3,
        out_specs=[pl.BlockSpec(memory_space=pltpu.VMEM)] * 2,
        scratch_shapes=[
            pltpu.VMEM(inputs.shape, bf16),
            pltpu.VMEM(cotangent.shape, bf16),
            pltpu.VMEM(kernel.shape, bf16),
            pltpu.VMEM((3 * LANES, 3 * LANES), bf16),
            pltpu.VMEM((all_frames, rows, across, own_out), bf16),
            pltpu.VMEM((groups, bands, own_in, positions), bf16),
            pltpu.VMEM((bands, own_in, positions), bf16),
            pltpu.VMEM((3, all_frames, plane + 2 * across, LANES), f32),
            pltpu.VMEM((all_frames, own_in, plane), f32),
            pltpu.VMEM((frames, own_in, plane), f32),
            pltpu.VMEM((bands, own_in, positions), f32),
            pltpu.VMEM((bands, own_in, positions), f32),
            pltpu.VMEM((all_frames + 2, 9 * own_in, plane), bf16),
            dma((3,)),
            dma((chips // 2, groups)),
            dma((chips // 2, groups)),
            dma((2, chips // 2, groups)),
            dma,
            dma,
            dma,
            dma,
            dma,
            dma,
            dma,
            dma,
            dma((frames,)),
            dma((frames,)),
            dma,
            dma,
        ],
        compiler_params=pltpu.CompilerParams(
            collective_id=0, has_side_effects=True, vmem_limit_bytes=60 * 2**20
        ),
    )(inputs, cotangent, kernel)


def local(inputs, cotangent, kernel):
    if exchange_fits(inputs, cotangent, kernel):
        return exchange_plan(inputs, cotangent, kernel)
    return gathered_plan(inputs, cotangent, kernel)


def solution(mesh):
    return jax.shard_map(
        local,
        mesh=mesh,
        in_specs=(P("tm", "rows", None, None), P("tm", "rows", None, None), P(None, "rows", "tm")),
        out_specs=(P("tm", "rows", None, None), P(None, "rows", "tm")),
        check_vma=False,
    )
```

```python
import functools

import jax
import jax.numpy as jnp
from jax import lax
from jax.experimental import pallas as pl
from jax.experimental.pallas import tpu as pltpu
from jax.sharding import PartitionSpec as P

MESH = pl.DeviceIdType.MESH
LANES = 128


def extended(block, sides, width):
    for axis, dim in sides:
        count = lax.axis_size(axis)
        forward = [(i, i + 1) for i in range(count - 1)]
        backward = [(target, source) for source, target in forward]
        low = lax.ppermute(
            lax.slice_in_dim(block, block.shape[dim] - width, None, axis=dim), axis, forward
        )
        high = lax.ppermute(lax.slice_in_dim(block, 0, width, axis=dim), axis, backward)
        block = jnp.concatenate([low, block, high], axis=dim)
    return block


def silu_slope(values):
    logistic = jax.nn.sigmoid(values)
    return logistic * (1.0 + values * (1.0 - logistic))


def widen_cols(values):
    return jnp.pad(values, ((0, 0), (0, 0), (1, 1), (0, 0)))


def tap_columns(padded, frames, height, across):
    pieces = []
    for time_tap in range(3):
        for row_tap in range(3):
            for col_tap in range(3):
                start_time, start_row, start_col = (2 - time_tap, 2 - row_tap, 2 - col_tap)
                pieces.append(
                    padded[
                        start_time : start_time + frames,
                        start_row : start_row + height,
                        start_col : start_col + across,
                    ]
                )
    stacked = jnp.stack(pieces, 3)
    return stacked.reshape(frames * height * across, 27, padded.shape[3])


def backward_piece(columns, portion):
    return lax.dot_general(
        columns, portion, (((1, 2), (0, 2)), ((), ())), preferred_element_type=jnp.float32
    )


def kernel_grad(haloed, gradient, factor):
    height = gradient.shape[1]
    across = gradient.shape[2]
    channels = haloed.shape[3]
    split_grads = lax.all_to_all(gradient, "tm", split_axis=3, concat_axis=0, tiled=True)
    width_out = split_grads.shape[3]
    padded_grads = jnp.pad(split_grads, ((0, 2), (0, 0), (0, 0), (0, 0)))
    portion = lax.all_gather(haloed, "tm", axis=0, tiled=True)
    offset = jnp.int32(0)
    portion_frames = portion.shape[0]
    widened = widen_cols(portion)
    spatial = jnp.stack(
        [
            widened[:, row_tap : row_tap + height, col_tap : col_tap + across]
            for row_tap in range(3)
            for col_tap in range(3)
        ],
        3,
    )
    shifted_grads = jnp.stack(
        [
            lax.dynamic_slice_in_dim(padded_grads, offset + 2 - time_tap, portion_frames, 0)
            for time_tap in range(3)
        ],
        0,
    )
    contribution = lax.dot_general(
        spatial,
        shifted_grads,
        (((0, 1, 2), (1, 2, 3)), ((), ())),
        preferred_element_type=jnp.float32,
    )
    contribution = jnp.transpose(contribution, (2, 0, 1, 3)).reshape(27, channels, width_out)
    return lax.psum_scatter(contribution * factor, "rows", scatter_dimension=1, tiled=True)


def gathered_plan(inputs, cotangent, kernel):
    frames, height, across, channels = inputs.shape
    positions = frames * height * across
    rows_kernel = lax.all_gather(kernel, "rows", axis=1, tiled=True)
    act = jax.nn.silu(inputs.astype(jnp.float32)).astype(jnp.bfloat16)
    paired = jnp.concatenate([act, cotangent], 3)
    paired_rows = extended(paired, (("rows", 1),), 1)
    halo_act = paired_rows[:, :, :, :channels]
    halo_grad = paired_rows[:, :, :, channels:]
    split_bands = lax.all_to_all(halo_grad, "tm", split_axis=3, concat_axis=0, tiled=True)
    total_frames = split_bands.shape[0]
    padded_bands = jnp.pad(split_bands, ((0, 2), (0, 0), (0, 0), (0, 0)))
    cols_all = tap_columns(widen_cols(padded_bands), total_frames, height, across)
    partial_terms = backward_piece(cols_all, rows_kernel).reshape(
        total_frames // frames, positions, channels
    )
    grad_act = lax.psum_scatter(partial_terms, "tm", scatter_dimension=0, tiled=True)
    grad_act = grad_act.reshape(frames, height, across, channels)
    grad_inputs = (
        cotangent.astype(jnp.float32) + grad_act * silu_slope(inputs.astype(jnp.float32))
    ).astype(jnp.bfloat16)
    factor = float(frames * lax.axis_size("tm") * height * lax.axis_size("rows") * across) ** (-0.5)
    grad_kernel = kernel_grad(halo_act, cotangent, factor)
    return (grad_inputs, grad_kernel)


def exchange_fits(inputs, cotangent, kernel):
    frames, height, across, channels = inputs.shape
    groups, bands = lax.axis_size("tm"), lax.axis_size("rows")
    own_in, own_out = kernel.shape[1], kernel.shape[2]
    return (
        frames == 2
        and frames * height * across == LANES
        and across == 16
        and own_in == 16
        and own_out == LANES
        and groups == 2
        and bands == 16
        and channels == own_in * bands == own_out * groups
        and frames * groups * height * bands * across * own_out * 2 <= 4 * 2**20
    )


def exchange_kernel(
    groups, bands, factor,
    inputs_hbm, cot_hbm, kernel_hbm, grad_in_ref, grad_kernel_ref,
    inputs_ref, cot_ref, taps_ref, turned, grads, acts, act_edge, act_send, sums, part_send, part,
    back_send, back, spatial, share, share_in,
    load_sem, line_recv, side_recv, edge_recv, taps_recv, line_send, side_send, edge_send, taps_send,
    act_send_sem, act_recv_sem, act_edge_send, act_edge_recv, cross_send_sem, cross_recv_sem,
    part_send_sem, part_recv_sem, back_send_sem, back_recv_sem, share_send, share_recv,
):
    frames, height, across, channels = inputs_ref.shape
    own_in = grad_kernel_ref.shape[1]
    pair_in = 2 * own_in
    positions = frames * height * across
    chips = bands // 2
    depth = chips // 2
    near = bands // 2
    rows = height * near
    plane = rows * across
    all_frames = frames * groups
    half = LANES // 2

    group, band = lax.axis_index("tm"), lax.axis_index("rows")
    partner = (group + 1) % groups
    chip, core = band // 2, band % 2
    layer, column = chip // 2, chip % 2
    keeper = layer // 2
    at_home = keeper == core
    other_core = (group, chip * 2 + 1 - core)

    def device_of(layer_of, column_of, core_of):
        return (layer_of * 2 + column_of) * 2 + core_of

    def region(group_of, near_band):
        return grads.at[pl.ds(group_of * frames, frames), pl.ds(1 + near_band * height, height)]

    def wait_bytes(ref, sem):
        pltpu.make_async_copy(ref, ref, sem).wait()

    def remote(source, target, send_sem, recv_sem, device):
        return pltpu.make_async_remote_copy(
            src_ref=source, dst_ref=target, send_sem=send_sem, recv_sem=recv_sem,
            device_id=device, device_id_type=MESH,
        )

    load_inputs = pltpu.make_async_copy(inputs_hbm, inputs_ref, load_sem.at[0])
    load_cot = pltpu.make_async_copy(cot_hbm, cot_ref, load_sem.at[1])
    load_kernel = pltpu.make_async_copy(kernel_hbm, taps_ref.at[core], load_sem.at[2])
    load_inputs.start()
    load_cot.start()
    load_kernel.start()

    barrier = pltpu.get_barrier_semaphore()

    def greet(step, carry):
        pl.semaphore_signal(
            barrier, inc=1, device_id=(group, (band + step) % bands), device_id_type=MESH
        )
        return carry

    def greet_column(step, carry):
        pl.semaphore_signal(
            barrier, inc=1, device_id=(partner, device_of(step // 2, column, step % 2)),
            device_id_type=MESH,
        )
        return carry

    lax.fori_loop(1, bands, greet, 0)
    lax.fori_loop(0, 2 * depth, greet_column, 0)
    pl.semaphore_wait(barrier, bands - 1 + 2 * depth)

    own_part = cot_hbm.at[:, :, :, pl.ds(pl.multiple_of(group * LANES, LANES), LANES)]
    other_part = cot_hbm.at[:, :, :, pl.ds(pl.multiple_of(partner * LANES, LANES), LANES)]
    landing = region(group, band % near)

    def send_line(turn, carry):
        layer_of = (layer // 2 + turn // 2) % 2 * 2 + (layer + turn) % 2
        target = device_of(layer_of, column, keeper)
        arrival = line_recv.at[layer % 2, core]

        @pl.when(target == band)
        def _():
            pltpu.make_async_copy(own_part, landing, arrival.at[0]).start()

        @pl.when(target != band)
        def _():
            remote(own_part, landing, line_send, arrival.at[0], (group, target)).start()

        remote(other_part, landing, line_send, arrival.at[1], (partner, target)).start()
        return carry

    lax.fori_loop(0, depth, send_line, 0)
    load_kernel.wait()
    remote(taps_ref.at[core], taps_ref.at[core], taps_send, taps_recv, other_core).start()

    load_inputs.wait()
    values = inputs_ref[...].reshape(positions, channels).astype(jnp.float32)
    act = values * jax.nn.sigmoid(values)
    act_send[...] = act.T.astype(jnp.bfloat16).reshape(chips, pair_in, positions)

    def send_act(step, carry):
        to_chip = (chip + step) % chips
        target = to_chip * 2 + keeper
        source, place = act_send.at[to_chip], acts.at[group, band % near]

        @pl.when(target == band)
        def _():
            pltpu.make_async_copy(source, place, act_recv_sem).start()

        @pl.when(target != band)
        def _():
            remote(source, place, act_send_sem, act_recv_sem, (group, target)).start()

        return carry

    lax.fori_loop(0, chips, send_act, 0)

    lane = lax.broadcasted_iota(jnp.int32, (pair_in, plane), 1)
    col = lane % across
    low = lax.broadcasted_iota(jnp.int32, (pair_in, LANES), 1) < half

    def moved(block, by_col):
        if by_col == 0:
            return block
        cells = col[:, : block.shape[1]] + by_col
        block = pltpu.roll(block, (-by_col) % block.shape[1], 1)
        return jnp.where((cells >= 0) & (cells < across), block, 0.0)

    wait_bytes(taps_ref.at[1 - core], taps_recv)
    wide = 3 * own_in
    for time_tap in range(3):
        for row_tap in range(3):
            at = pl.ds(9 * time_tap + 3 * row_tap, 3)
            block = jnp.concatenate(
                [taps_ref[0, at].reshape(wide, LANES), taps_ref[1, at].reshape(wide, LANES)]
            ).astype(jnp.float32)
            block = jnp.concatenate([block, jnp.zeros((LANES - 2 * wide, LANES), jnp.float32)])
            turned[pl.ds(time_tap * LANES, LANES), pl.ds(row_tap * LANES, LANES)] = (
                block.T.astype(jnp.bfloat16)
            )
    spatial[pl.ds(0, 2)] = jnp.zeros((2,) + spatial.shape[1:], spatial.dtype)
    grads[:, pl.ds((rows + 1) * core, 1)] = jnp.zeros((all_frames, 1, across, LANES), jnp.bfloat16)

    def sum_rows(first, count):
        cells = [
            grads[frame, pl.ds(first, count)].reshape(count * across, LANES)
            for frame in range(all_frames)
        ] + [jnp.zeros((count * across, LANES), jnp.bfloat16)] * 2
        windows = jnp.concatenate(
            [
                jnp.concatenate([cells[frame + 2 - tap] for tap in range(3)], axis=1)
                for frame in range(all_frames)
            ],
            axis=0,
        )
        result = lax.dot_general(
            windows, turned[...], (((1,), (0,)), ((), ())), preferred_element_type=jnp.float32
        ).reshape(all_frames, count * across, 3 * LANES)
        start = first * across
        if not isinstance(start, int):
            start = pl.multiple_of(start, across)
        for row_tap in range(3):
            sums[row_tap, :, pl.ds(start, count * across)] = result[
                :, :, row_tap * LANES : (row_tap + 1) * LANES
            ]

    def all_of(near_band):
        return grads.at[:, pl.ds(1 + near_band * height, height)]

    def pass_line(turn):
        odd = (layer + turn) % 2
        for core_of in range(2):
            near_band = odd * 4 + column * 2 + core_of
            for piece in range(groups):
                wait_bytes(region((group + piece) % groups, near_band),
                           line_recv.at[odd, core_of, piece])
            remote(
                all_of(near_band), all_of(near_band), side_send, side_recv.at[odd, core_of],
                (group, device_of(layer, 1 - column, core)),
            ).start()
        sum_rows(1 + (odd * 2 + column) * 2 * height, 2 * height)

    def take_side(turn):
        odd = (layer + turn) % 2
        for core_of in range(2):
            near_band = odd * 4 + (1 - column) * 2 + core_of
            wait_bytes(all_of(near_band), side_recv.at[odd, core_of])
        sum_rows(1 + (odd * 2 + 1 - column) * 2 * height, 2 * height)

    def pass_lines(turn, carry):
        pass_line(turn)
        return carry

    lax.fori_loop(0, 2, pass_lines, 0)

    wait_bytes(acts.at[group], act_recv_sem)
    remote(
        acts.at[group], acts.at[group], cross_send_sem, cross_recv_sem, (partner, band)
    ).start()

    def take_sides(turn, carry):
        take_side(turn)
        return carry

    lax.fori_loop(0, 2, take_sides, 0)
    edge_from = grads.at[:, pl.ds((1 - core) * rows + core, 1)]
    edge_to = grads.at[:, pl.ds(core * (rows + 1), 1)]
    edge_in = grads.at[:, pl.ds((1 - core) * (rows + 1), 1)]
    remote(edge_from, edge_to, edge_send, edge_recv, other_core).start()
    wait_bytes(edge_in, edge_recv)
    sum_rows(0, 1)
    sum_rows(rows + 1, 1)

    def grad_act_of(frame):
        mixed = None
        for row_tap in range(3):
            term = sums[row_tap, frame, pl.ds(across * (2 - row_tap), plane)]
            mixed = term if mixed is None else mixed + term
        mixed = mixed.T
        result = None
        for col_tap in range(3):
            at = col_tap * own_in
            term = jnp.concatenate([mixed[at : at + own_in], mixed[wide + at : wide + at + own_in]])
            term = moved(term, 1 - col_tap)
            result = term if result is None else result + term
        return result

    def shares(at, carry):
        owner = (partner + at // frames) % groups
        part_send[at] = grad_act_of(owner * frames + at % frames)

        @pl.when(at < frames)
        def _():
            remote(
                part_send.at[at], part.at[at], part_send_sem.at[at], part_recv_sem.at[at],
                (partner, band),
            ).start()

        return carry

    lax.fori_loop(0, all_frames, shares, 0)

    wait_bytes(acts.at[partner], cross_recv_sem)
    remote(
        acts.at[:, (1 - core) * (near - 1)], act_edge, act_edge_send, act_edge_recv, other_core
    ).start()
    for at in range(frames):
        wait_bytes(part.at[at], part_recv_sem.at[at])
    first, second = [part_send[frames + at] + part[at] for at in range(frames)]
    for pair in range(near // 2):
        x = first[:, pair * LANES : (pair + 1) * LANES]
        y = second[:, pair * LANES : (pair + 1) * LANES]
        back_send[2 * pair] = jnp.where(low, x, pltpu.roll(y, half, 1))
        back_send[2 * pair + 1] = jnp.where(low, pltpu.roll(x, half, 1), y)

    def send_back(step, carry):
        near_band = (band + step) % near
        target = core * near + near_band
        source, place = back_send.at[near_band], back.at[chip]

        @pl.when(target == band)
        def _():
            pltpu.make_async_copy(source, place, back_recv_sem).start()

        @pl.when(target != band)
        def _():
            remote(source, place, back_send_sem, back_recv_sem, (group, target)).start()

        return carry

    lax.fori_loop(0, near, send_back, 0)

    wait_bytes(act_edge, act_edge_recv)

    def shift_acts(group_of, carry):
        edge_tile = act_edge[group_of].astype(jnp.float32)
        above = jnp.where(core == 1, edge_tile, 0.0)
        below = jnp.where(core == 0, edge_tile, 0.0)
        for at in range(frames):
            tiles = []
            for pair in range(near // 2):
                x = acts[group_of, 2 * pair].astype(jnp.float32)
                y = acts[group_of, 2 * pair + 1].astype(jnp.float32)
                if at == 0:
                    tiles.append(jnp.where(low, x, pltpu.roll(y, half, 1)))
                else:
                    tiles.append(jnp.where(low, pltpu.roll(x, half, 1), y))
            whole = jnp.concatenate(tiles, axis=1)
            for col_tap in range(3):
                shifted = moved(whole, col_tap - 1)
                top = pltpu.roll(moved(above, col_tap - 1), (2 * LANES - at * half - 48) % LANES, 1)
                end = pltpu.roll(moved(below, col_tap - 1), (2 * LANES - at * half - across) % LANES, 1)
                repeat = plane // LANES
                top = jnp.concatenate([top] * repeat, axis=1)
                end = jnp.concatenate([end] * repeat, axis=1)
                up = jnp.where(lane < across, top, pltpu.roll(shifted, across, 1))
                down = jnp.where(lane >= plane - across, end, pltpu.roll(shifted, plane - across, 1))
                for row_tap, block in enumerate((up, shifted, down)):
                    tap = 3 * row_tap + col_tap
                    spatial[2 + group_of * frames + at, pl.ds(tap * pair_in, pair_in)] = (
                        block.astype(jnp.bfloat16)
                    )
        return carry

    lax.fori_loop(0, groups, shift_acts, 0)
    share[...] = jnp.zeros_like(share)

    def kernel_taps(frame, carry):
        cells = grads[frame, pl.ds(1, rows)].reshape(plane, LANES)
        for time_tap in range(3):
            term = lax.dot_general(
                spatial[frame + time_tap], cells, (((1,), (0,)), ((), ())),
                preferred_element_type=jnp.float32,
            ).reshape(9, 2, own_in, LANES)
            own = pl.ds(9 * time_tap, 9)
            for core_of in range(2):
                share[core_of, own] = share[core_of, own] + term[:, core_of]
        return carry

    lax.fori_loop(0, all_frames, kernel_taps, 0)
    remote(share.at[1 - core], share_in, share_send, share_recv, other_core).start()

    wait_bytes(back, back_recv_sem)
    grad_act = back[...].reshape(channels, positions).T
    values = inputs_ref[...].reshape(positions, channels).astype(jnp.float32)
    load_cot.wait()
    cot = cot_ref[...].reshape(positions, channels).astype(jnp.float32)
    grad_in = cot + grad_act * silu_slope(values)
    grad_in_ref[...] = grad_in.astype(jnp.bfloat16).reshape(grad_in_ref.shape)
    wait_bytes(share_in, share_recv)
    grad_kernel_ref[...] = (share[core] + share_in[...]) * factor

    sent = 2 * depth

    @pl.when(at_home)
    def _():
        wait_bytes(grads.at[pl.ds(0, frames), pl.ds(0, height * (sent - 1))], line_send)
        wait_bytes(acts.at[0, pl.ds(0, chips - 1)], act_send_sem)
        wait_bytes(back.at[pl.ds(0, near - 1)], back_send_sem)

    @pl.when(jnp.logical_not(at_home))
    def _():
        wait_bytes(grads.at[pl.ds(0, frames), pl.ds(0, height * sent)], line_send)
        wait_bytes(acts.at[0, pl.ds(0, chips)], act_send_sem)
        wait_bytes(back.at[pl.ds(0, near)], back_send_sem)

    wait_bytes(grads.at[:, pl.ds(0, 4 * height)], side_send)
    wait_bytes(edge_from, edge_send)
    wait_bytes(taps_ref.at[core], taps_send)
    wait_bytes(act_edge, act_edge_send)
    wait_bytes(acts.at[group], cross_send_sem)
    for at in range(frames):
        wait_bytes(part_send.at[at], part_send_sem.at[at])
    wait_bytes(share_in, share_send)


def exchange_plan(inputs, cotangent, kernel):
    frames, height, across, channels = inputs.shape
    taps, own_in, own_out = kernel.shape
    groups, bands = lax.axis_size("tm"), lax.axis_size("rows")
    positions = frames * height * across
    all_frames, chips, near = frames * groups, bands // 2, bands // 2
    rows = height * near
    plane = rows * across
    factor = float(all_frames * 2 * plane) ** (-0.5)
    dma = pltpu.SemaphoreType.DMA
    bf16, f32 = jnp.bfloat16, jnp.float32
    return pl.pallas_call(
        functools.partial(exchange_kernel, groups, bands, factor),
        out_shape=(pltpu.VMEM(inputs.shape, bf16), pltpu.VMEM(kernel.shape, f32)),
        in_specs=[pl.BlockSpec(memory_space=pltpu.HBM)] * 3,
        out_specs=[pl.BlockSpec(memory_space=pltpu.VMEM)] * 2,
        scratch_shapes=[
            pltpu.VMEM(inputs.shape, bf16),
            pltpu.VMEM(cotangent.shape, bf16),
            pltpu.VMEM((2,) + kernel.shape, bf16),
            pltpu.VMEM((3 * LANES, 3 * LANES), bf16),
            pltpu.VMEM((all_frames, rows + 2, across, own_out), bf16),
            pltpu.VMEM((groups, near, 2 * own_in, positions), bf16),
            pltpu.VMEM((groups, 2 * own_in, positions), bf16),
            pltpu.VMEM((chips, 2 * own_in, positions), bf16),
            pltpu.VMEM((3, all_frames, plane + 2 * across, LANES), f32),
            pltpu.VMEM((all_frames, 2 * own_in, plane), f32),
            pltpu.VMEM((frames, 2 * own_in, plane), f32),
            pltpu.VMEM((near, 2 * own_in, positions), f32),
            pltpu.VMEM((chips, 2 * own_in, positions), f32),
            pltpu.VMEM((all_frames + 2, 18 * own_in, plane), bf16),
            pltpu.VMEM((2,) + kernel.shape, f32),
            pltpu.VMEM(kernel.shape, f32),
            dma((3,)),
            dma((2, 2, groups)),
            dma((2, 2)),
        ] + [dma] * 12 + [dma((frames,))] * 2 + [dma] * 4,
        compiler_params=pltpu.CompilerParams(
            collective_id=0, has_side_effects=True, vmem_limit_bytes=60 * 2**20
        ),
    )(inputs, cotangent, kernel)


def local(inputs, cotangent, kernel):
    if exchange_fits(inputs, cotangent, kernel):
        return exchange_plan(inputs, cotangent, kernel)
    return gathered_plan(inputs, cotangent, kernel)


def solution(mesh):
    return jax.shard_map(
        local,
        mesh=mesh,
        in_specs=(P("tm", "rows", None, None), P("tm", "rows", None, None), P(None, "rows", "tm")),
        out_specs=(P("tm", "rows", None, None), P(None, "rows", "tm")),
        check_vma=False,
    )
```

```python
import functools

import jax
import jax.numpy as jnp
from jax import lax
from jax.experimental import pallas as pl
from jax.experimental.pallas import tpu as pltpu
from jax.sharding import PartitionSpec as P

MESH = pl.DeviceIdType.MESH
LANES = 128


def extended(block, sides, width):
    for axis, dim in sides:
        count = lax.axis_size(axis)
        forward = [(i, i + 1) for i in range(count - 1)]
        backward = [(target, source) for source, target in forward]
        low = lax.ppermute(
            lax.slice_in_dim(block, block.shape[dim] - width, None, axis=dim), axis, forward
        )
        high = lax.ppermute(lax.slice_in_dim(block, 0, width, axis=dim), axis, backward)
        block = jnp.concatenate([low, block, high], axis=dim)
    return block


def silu_slope(values):
    logistic = jax.nn.sigmoid(values)
    return logistic * (1.0 + values * (1.0 - logistic))


def widen_cols(values):
    return jnp.pad(values, ((0, 0), (0, 0), (1, 1), (0, 0)))


def tap_columns(padded, frames, height, across):
    pieces = []
    for time_tap in range(3):
        for row_tap in range(3):
            for col_tap in range(3):
                start_time, start_row, start_col = (2 - time_tap, 2 - row_tap, 2 - col_tap)
                pieces.append(
                    padded[
                        start_time : start_time + frames,
                        start_row : start_row + height,
                        start_col : start_col + across,
                    ]
                )
    stacked = jnp.stack(pieces, 3)
    return stacked.reshape(frames * height * across, 27, padded.shape[3])


def backward_piece(columns, portion):
    return lax.dot_general(
        columns, portion, (((1, 2), (0, 2)), ((), ())), preferred_element_type=jnp.float32
    )


def kernel_grad(haloed, gradient, factor):
    height = gradient.shape[1]
    across = gradient.shape[2]
    channels = haloed.shape[3]
    split_grads = lax.all_to_all(gradient, "tm", split_axis=3, concat_axis=0, tiled=True)
    width_out = split_grads.shape[3]
    padded_grads = jnp.pad(split_grads, ((0, 2), (0, 0), (0, 0), (0, 0)))
    portion = lax.all_gather(haloed, "tm", axis=0, tiled=True)
    offset = jnp.int32(0)
    portion_frames = portion.shape[0]
    widened = widen_cols(portion)
    spatial = jnp.stack(
        [
            widened[:, row_tap : row_tap + height, col_tap : col_tap + across]
            for row_tap in range(3)
            for col_tap in range(3)
        ],
        3,
    )
    shifted_grads = jnp.stack(
        [
            lax.dynamic_slice_in_dim(padded_grads, offset + 2 - time_tap, portion_frames, 0)
            for time_tap in range(3)
        ],
        0,
    )
    contribution = lax.dot_general(
        spatial,
        shifted_grads,
        (((0, 1, 2), (1, 2, 3)), ((), ())),
        preferred_element_type=jnp.float32,
    )
    contribution = jnp.transpose(contribution, (2, 0, 1, 3)).reshape(27, channels, width_out)
    return lax.psum_scatter(contribution * factor, "rows", scatter_dimension=1, tiled=True)


def gathered_plan(inputs, cotangent, kernel):
    frames, height, across, channels = inputs.shape
    positions = frames * height * across
    rows_kernel = lax.all_gather(kernel, "rows", axis=1, tiled=True)
    act = jax.nn.silu(inputs.astype(jnp.float32)).astype(jnp.bfloat16)
    paired = jnp.concatenate([act, cotangent], 3)
    paired_rows = extended(paired, (("rows", 1),), 1)
    halo_act = paired_rows[:, :, :, :channels]
    halo_grad = paired_rows[:, :, :, channels:]
    split_bands = lax.all_to_all(halo_grad, "tm", split_axis=3, concat_axis=0, tiled=True)
    total_frames = split_bands.shape[0]
    padded_bands = jnp.pad(split_bands, ((0, 2), (0, 0), (0, 0), (0, 0)))
    cols_all = tap_columns(widen_cols(padded_bands), total_frames, height, across)
    partial_terms = backward_piece(cols_all, rows_kernel).reshape(
        total_frames // frames, positions, channels
    )
    grad_act = lax.psum_scatter(partial_terms, "tm", scatter_dimension=0, tiled=True)
    grad_act = grad_act.reshape(frames, height, across, channels)
    grad_inputs = (
        cotangent.astype(jnp.float32) + grad_act * silu_slope(inputs.astype(jnp.float32))
    ).astype(jnp.bfloat16)
    factor = float(frames * lax.axis_size("tm") * height * lax.axis_size("rows") * across) ** (-0.5)
    grad_kernel = kernel_grad(halo_act, cotangent, factor)
    return (grad_inputs, grad_kernel)


def exchange_fits(inputs, cotangent, kernel):
    frames, height, across, channels = inputs.shape
    groups, bands = lax.axis_size("tm"), lax.axis_size("rows")
    own_in, own_out = kernel.shape[1], kernel.shape[2]
    return (
        frames == 2
        and frames * height * across == LANES
        and across == 16
        and own_in == 16
        and own_out == LANES
        and groups == 2
        and bands == 16
        and channels == own_in * bands == own_out * groups
        and frames * groups * height * bands * across * own_out * 2 <= 4 * 2**20
    )


def exchange_kernel(
    groups, bands, factor,
    inputs_hbm, cot_hbm, kernel_hbm, grad_in_ref, grad_kernel_ref,
    inputs_ref, cot_ref, taps_ref, turned, grads, acts, act_edge, act_send, sums, part_send, part,
    back_send, back, spatial, share, share_in,
    load_sem, line_recv, side_recv, edge_recv, taps_recv, line_send, side_send, edge_send, taps_send,
    act_send_sem, act_recv_sem, act_edge_send, act_edge_recv, cross_send_sem, cross_recv_sem,
    part_send_sem, part_recv_sem, back_send_sem, back_recv_sem, share_send, share_recv,
):
    frames, height, across, channels = inputs_ref.shape
    own_in = grad_kernel_ref.shape[1]
    pair_in = 2 * own_in
    positions = frames * height * across
    chips = bands // 2
    depth = chips // 2
    near = bands // 2
    rows = height * near
    plane = rows * across
    all_frames = frames * groups
    half = LANES // 2

    group, band = lax.axis_index("tm"), lax.axis_index("rows")
    partner = (group + 1) % groups
    chip, core = band // 2, band % 2
    layer, column = chip // 2, chip % 2
    keeper = layer // 2
    at_home = keeper == core
    other_core = (group, chip * 2 + 1 - core)

    def device_of(layer_of, column_of, core_of):
        return (layer_of * 2 + column_of) * 2 + core_of

    def region(group_of, near_band):
        return grads.at[pl.ds(group_of * frames, frames), pl.ds(1 + near_band * height, height)]

    def wait_bytes(ref, sem):
        pltpu.make_async_copy(ref, ref, sem).wait()

    def remote(source, target, send_sem, recv_sem, device):
        return pltpu.make_async_remote_copy(
            src_ref=source, dst_ref=target, send_sem=send_sem, recv_sem=recv_sem,
            device_id=device, device_id_type=MESH,
        )

    load_inputs = pltpu.make_async_copy(inputs_hbm, inputs_ref, load_sem.at[0])
    load_cot = pltpu.make_async_copy(cot_hbm, cot_ref, load_sem.at[1])
    load_kernel = pltpu.make_async_copy(kernel_hbm, taps_ref.at[core], load_sem.at[2])
    load_inputs.start()
    load_cot.start()
    load_kernel.start()

    barrier = pltpu.get_barrier_semaphore()

    def greet(step, carry):
        pl.semaphore_signal(
            barrier, inc=1, device_id=(group, (band + step) % bands), device_id_type=MESH
        )
        return carry

    def greet_column(step, carry):
        pl.semaphore_signal(
            barrier, inc=1, device_id=(partner, device_of(step // 2, column, step % 2)),
            device_id_type=MESH,
        )
        return carry

    lax.fori_loop(1, bands, greet, 0)
    lax.fori_loop(0, 2 * depth, greet_column, 0)
    pl.semaphore_wait(barrier, bands - 1 + 2 * depth)

    own_part = cot_hbm.at[:, :, :, pl.ds(pl.multiple_of(group * LANES, LANES), LANES)]
    other_part = cot_hbm.at[:, :, :, pl.ds(pl.multiple_of(partner * LANES, LANES), LANES)]
    landing = region(group, band % near)

    def send_line(turn, carry):
        layer_of = (layer // 2 + turn // 2) % 2 * 2 + (layer + turn) % 2
        target = device_of(layer_of, column, keeper)
        arrival = line_recv.at[layer % 2, core]

        @pl.when(target == band)
        def _():
            pltpu.make_async_copy(own_part, landing, arrival.at[0]).start()

        @pl.when(target != band)
        def _():
            remote(own_part, landing, line_send, arrival.at[0], (group, target)).start()

        remote(other_part, landing, line_send, arrival.at[1], (partner, target)).start()
        return carry

    lax.fori_loop(0, depth, send_line, 0)
    load_kernel.wait()
    remote(taps_ref.at[core], taps_ref.at[core], taps_send, taps_recv, other_core).start()

    load_inputs.wait()
    values = inputs_ref[...].reshape(positions, channels).astype(jnp.float32)
    act = values * jax.nn.sigmoid(values)
    act_send[...] = act.T.astype(jnp.bfloat16).reshape(chips, pair_in, positions)

    def send_act(step, carry):
        to_chip = (chip + step) % chips
        target = to_chip * 2 + keeper
        source, place = act_send.at[to_chip], acts.at[group, band % near]

        @pl.when(target == band)
        def _():
            pltpu.make_async_copy(source, place, act_recv_sem).start()

        @pl.when(target != band)
        def _():
            remote(source, place, act_send_sem, act_recv_sem, (group, target)).start()

        return carry

    lax.fori_loop(0, chips, send_act, 0)

    lane = lax.broadcasted_iota(jnp.int32, (pair_in, plane), 1)
    col = lane % across
    low = lax.broadcasted_iota(jnp.int32, (pair_in, LANES), 1) < half

    def moved(block, by_col):
        if by_col == 0:
            return block
        cells = col[:, : block.shape[1]] + by_col
        block = pltpu.roll(block, (-by_col) % block.shape[1], 1)
        return jnp.where((cells >= 0) & (cells < across), block, 0.0)

    wait_bytes(taps_ref.at[1 - core], taps_recv)
    wide = 3 * own_in
    for time_tap in range(3):
        for row_tap in range(3):
            at = pl.ds(9 * time_tap + 3 * row_tap, 3)
            block = jnp.concatenate(
                [taps_ref[0, at].reshape(wide, LANES), taps_ref[1, at].reshape(wide, LANES)]
            ).astype(jnp.float32)
            block = jnp.concatenate([block, jnp.zeros((LANES - 2 * wide, LANES), jnp.float32)])
            turned[pl.ds(time_tap * LANES, LANES), pl.ds(row_tap * LANES, LANES)] = (
                block.T.astype(jnp.bfloat16)
            )
    spatial[pl.ds(0, 2)] = jnp.zeros((2,) + spatial.shape[1:], spatial.dtype)
    grads[:, pl.ds((rows + 1) * core, 1)] = jnp.zeros((all_frames, 1, across, LANES), jnp.bfloat16)

    def sum_rows(first, count):
        cells = [
            grads[frame, pl.ds(first, count)].reshape(count * across, LANES)
            for frame in range(all_frames)
        ] + [jnp.zeros((count * across, LANES), jnp.bfloat16)] * 2
        windows = jnp.concatenate(
            [
                jnp.concatenate([cells[frame + 2 - tap] for tap in range(3)], axis=1)
                for frame in range(all_frames)
            ],
            axis=0,
        )
        result = lax.dot_general(
            windows, turned[...], (((1,), (0,)), ((), ())), preferred_element_type=jnp.float32
        ).reshape(all_frames, count * across, 3 * LANES)
        start = first * across
        if not isinstance(start, int):
            start = pl.multiple_of(start, across)
        for row_tap in range(3):
            sums[row_tap, :, pl.ds(start, count * across)] = result[
                :, :, row_tap * LANES : (row_tap + 1) * LANES
            ]

    def all_of(near_band):
        return grads.at[:, pl.ds(1 + near_band * height, height)]

    edge_from = grads.at[:, pl.ds((1 - core) * rows + core, 1)]
    edge_to = grads.at[:, pl.ds(core * (rows + 1), 1)]
    edge_in = grads.at[:, pl.ds((1 - core) * (rows + 1), 1)]

    def pass_edge(near_band):
        @pl.when(near_band == (1 - core) * (near - 1))
        def _():
            remote(edge_from, edge_to, edge_send, edge_recv, other_core).start()

    def pass_line(turn, carry):
        odd = (layer + turn) % 2
        for core_of in range(2):
            near_band = odd * 4 + column * 2 + core_of
            for piece in range(groups):
                wait_bytes(region((group + piece) % groups, near_band),
                           line_recv.at[odd, core_of, piece])
            remote(
                all_of(near_band), all_of(near_band), side_send, side_recv.at[odd, core_of],
                (group, device_of(layer, 1 - column, core)),
            ).start()
            pass_edge(near_band)
        return carry

    def take_side(turn):
        odd = (layer + turn) % 2
        for core_of in range(2):
            near_band = odd * 4 + (1 - column) * 2 + core_of
            wait_bytes(all_of(near_band), side_recv.at[odd, core_of])
            pass_edge(near_band)

    lax.fori_loop(0, 2, pass_line, 0)

    wait_bytes(acts.at[group], act_recv_sem)
    remote(
        acts.at[group], acts.at[group], cross_send_sem, cross_recv_sem, (partner, band)
    ).start()

    def sum_chips(turn, carry):
        odd = (layer + turn) % 2
        far = turn // 2

        @pl.when(far == 1)
        def _():
            take_side(turn)

        sum_rows(1 + (odd * 2 + column + far - 2 * column * far) * 2 * height, 2 * height)
        return carry

    lax.fori_loop(0, 4, sum_chips, 0)

    wait_bytes(acts.at[partner], cross_recv_sem)
    remote(
        acts.at[:, (1 - core) * (near - 1)], act_edge, act_edge_send, act_edge_recv, other_core
    ).start()
    wait_bytes(edge_in, edge_recv)
    sum_rows(0, 1)
    sum_rows(rows + 1, 1)

    def grad_act_of(frame):
        mixed = None
        for row_tap in range(3):
            term = sums[row_tap, frame, pl.ds(across * (2 - row_tap), plane)]
            mixed = term if mixed is None else mixed + term
        mixed = mixed.T
        result = None
        for col_tap in range(3):
            at = col_tap * own_in
            term = jnp.concatenate([mixed[at : at + own_in], mixed[wide + at : wide + at + own_in]])
            term = moved(term, 1 - col_tap)
            result = term if result is None else result + term
        return result

    def shares(at, carry):
        owner = (partner + at // frames) % groups
        part_send[at] = grad_act_of(owner * frames + at % frames)

        @pl.when(at < frames)
        def _():
            remote(
                part_send.at[at], part.at[at], part_send_sem.at[at], part_recv_sem.at[at],
                (partner, band),
            ).start()

        return carry

    lax.fori_loop(0, all_frames, shares, 0)

    wait_bytes(act_edge, act_edge_recv)

    def shift_acts(group_of, carry):
        edge_tile = act_edge[group_of].astype(jnp.float32)
        above = jnp.where(core == 1, edge_tile, 0.0)
        below = jnp.where(core == 0, edge_tile, 0.0)
        for at in range(frames):
            tiles = []
            for pair in range(near // 2):
                x = acts[group_of, 2 * pair].astype(jnp.float32)
                y = acts[group_of, 2 * pair + 1].astype(jnp.float32)
                if at == 0:
                    tiles.append(jnp.where(low, x, pltpu.roll(y, half, 1)))
                else:
                    tiles.append(jnp.where(low, pltpu.roll(x, half, 1), y))
            whole = jnp.concatenate(tiles, axis=1)
            for col_tap in range(3):
                shifted = moved(whole, col_tap - 1)
                top = pltpu.roll(moved(above, col_tap - 1), (2 * LANES - at * half - 48) % LANES, 1)
                end = pltpu.roll(moved(below, col_tap - 1), (2 * LANES - at * half - across) % LANES, 1)
                repeat = plane // LANES
                top = jnp.concatenate([top] * repeat, axis=1)
                end = jnp.concatenate([end] * repeat, axis=1)
                up = jnp.where(lane < across, top, pltpu.roll(shifted, across, 1))
                down = jnp.where(lane >= plane - across, end, pltpu.roll(shifted, plane - across, 1))
                for row_tap, block in enumerate((up, shifted, down)):
                    tap = 3 * row_tap + col_tap
                    spatial[2 + group_of * frames + at, pl.ds(tap * pair_in, pair_in)] = (
                        block.astype(jnp.bfloat16)
                    )
        return carry

    lax.fori_loop(0, groups, shift_acts, 0)
    share[...] = jnp.zeros_like(share)

    for at in range(frames):
        wait_bytes(part.at[at], part_recv_sem.at[at])
    first, second = [part_send[frames + at] + part[at] for at in range(frames)]
    for pair in range(near // 2):
        x = first[:, pair * LANES : (pair + 1) * LANES]
        y = second[:, pair * LANES : (pair + 1) * LANES]
        back_send[2 * pair] = jnp.where(low, x, pltpu.roll(y, half, 1))
        back_send[2 * pair + 1] = jnp.where(low, pltpu.roll(x, half, 1), y)

    def send_back(step, carry):
        near_band = (band + step) % near
        target = core * near + near_band
        source, place = back_send.at[near_band], back.at[chip]

        @pl.when(target == band)
        def _():
            pltpu.make_async_copy(source, place, back_recv_sem).start()

        @pl.when(target != band)
        def _():
            remote(source, place, back_send_sem, back_recv_sem, (group, target)).start()

        return carry

    lax.fori_loop(0, near, send_back, 0)

    def kernel_taps(frame, carry):
        cells = grads[frame, pl.ds(1, rows)].reshape(plane, LANES)
        for time_tap in range(3):
            term = lax.dot_general(
                spatial[frame + time_tap], cells, (((1,), (0,)), ((), ())),
                preferred_element_type=jnp.float32,
            ).reshape(9, 2, own_in, LANES)
            own = pl.ds(9 * time_tap, 9)
            for core_of in range(2):
                share[core_of, own] = share[core_of, own] + term[:, core_of]
        return carry

    lax.fori_loop(0, all_frames, kernel_taps, 0)
    remote(share.at[1 - core], share_in, share_send, share_recv, other_core).start()

    wait_bytes(back, back_recv_sem)
    grad_act = back[...].reshape(channels, positions).T
    values = inputs_ref[...].reshape(positions, channels).astype(jnp.float32)
    load_cot.wait()
    cot = cot_ref[...].reshape(positions, channels).astype(jnp.float32)
    grad_in = cot + grad_act * silu_slope(values)
    grad_in_ref[...] = grad_in.astype(jnp.bfloat16).reshape(grad_in_ref.shape)
    wait_bytes(share_in, share_recv)
    grad_kernel_ref[...] = (share[core] + share_in[...]) * factor

    sent = 2 * depth

    @pl.when(at_home)
    def _():
        wait_bytes(grads.at[pl.ds(0, frames), pl.ds(0, height * (sent - 1))], line_send)
        wait_bytes(acts.at[0, pl.ds(0, chips - 1)], act_send_sem)
        wait_bytes(back.at[pl.ds(0, near - 1)], back_send_sem)

    @pl.when(jnp.logical_not(at_home))
    def _():
        wait_bytes(grads.at[pl.ds(0, frames), pl.ds(0, height * sent)], line_send)
        wait_bytes(acts.at[0, pl.ds(0, chips)], act_send_sem)
        wait_bytes(back.at[pl.ds(0, near)], back_send_sem)

    wait_bytes(grads.at[:, pl.ds(0, 4 * height)], side_send)
    wait_bytes(edge_from, edge_send)
    wait_bytes(taps_ref.at[core], taps_send)
    wait_bytes(act_edge, act_edge_send)
    wait_bytes(acts.at[group], cross_send_sem)
    for at in range(frames):
        wait_bytes(part_send.at[at], part_send_sem.at[at])
    wait_bytes(share_in, share_send)


def exchange_plan(inputs, cotangent, kernel):
    frames, height, across, channels = inputs.shape
    taps, own_in, own_out = kernel.shape
    groups, bands = lax.axis_size("tm"), lax.axis_size("rows")
    positions = frames * height * across
    all_frames, chips, near = frames * groups, bands // 2, bands // 2
    rows = height * near
    plane = rows * across
    factor = float(all_frames * 2 * plane) ** (-0.5)
    dma = pltpu.SemaphoreType.DMA
    bf16, f32 = jnp.bfloat16, jnp.float32
    return pl.pallas_call(
        functools.partial(exchange_kernel, groups, bands, factor),
        out_shape=(pltpu.VMEM(inputs.shape, bf16), pltpu.VMEM(kernel.shape, f32)),
        in_specs=[pl.BlockSpec(memory_space=pltpu.HBM)] * 3,
        out_specs=[pl.BlockSpec(memory_space=pltpu.VMEM)] * 2,
        scratch_shapes=[
            pltpu.VMEM(inputs.shape, bf16),
            pltpu.VMEM(cotangent.shape, bf16),
            pltpu.VMEM((2,) + kernel.shape, bf16),
            pltpu.VMEM((3 * LANES, 3 * LANES), bf16),
            pltpu.VMEM((all_frames, rows + 2, across, own_out), bf16),
            pltpu.VMEM((groups, near, 2 * own_in, positions), bf16),
            pltpu.VMEM((groups, 2 * own_in, positions), bf16),
            pltpu.VMEM((chips, 2 * own_in, positions), bf16),
            pltpu.VMEM((3, all_frames, plane + 2 * across, LANES), f32),
            pltpu.VMEM((all_frames, 2 * own_in, plane), f32),
            pltpu.VMEM((frames, 2 * own_in, plane), f32),
            pltpu.VMEM((near, 2 * own_in, positions), f32),
            pltpu.VMEM((chips, 2 * own_in, positions), f32),
            pltpu.VMEM((all_frames + 2, 18 * own_in, plane), bf16),
            pltpu.VMEM((2,) + kernel.shape, f32),
            pltpu.VMEM(kernel.shape, f32),
            dma((3,)),
            dma((2, 2, groups)),
            dma((2, 2)),
        ] + [dma] * 12 + [dma((frames,))] * 2 + [dma] * 4,
        compiler_params=pltpu.CompilerParams(
            collective_id=0, has_side_effects=True, vmem_limit_bytes=60 * 2**20
        ),
    )(inputs, cotangent, kernel)


def local(inputs, cotangent, kernel):
    if exchange_fits(inputs, cotangent, kernel):
        return exchange_plan(inputs, cotangent, kernel)
    return gathered_plan(inputs, cotangent, kernel)


def solution(mesh):
    return jax.shard_map(
        local,
        mesh=mesh,
        in_specs=(P("tm", "rows", None, None), P("tm", "rows", None, None), P(None, "rows", "tm")),
        out_specs=(P("tm", "rows", None, None), P(None, "rows", "tm")),
        check_vma=False,
    )
```

```python
import functools

import jax
import jax.numpy as jnp
from jax import lax
from jax.experimental import pallas as pl
from jax.experimental.pallas import tpu as pltpu
from jax.sharding import PartitionSpec as P

MESH = pl.DeviceIdType.MESH
LANES = 128


def extended(block, sides, width):
    for axis, dim in sides:
        count = lax.axis_size(axis)
        forward = [(i, i + 1) for i in range(count - 1)]
        backward = [(target, source) for source, target in forward]
        low = lax.ppermute(
            lax.slice_in_dim(block, block.shape[dim] - width, None, axis=dim), axis, forward
        )
        high = lax.ppermute(lax.slice_in_dim(block, 0, width, axis=dim), axis, backward)
        block = jnp.concatenate([low, block, high], axis=dim)
    return block


def silu_slope(values):
    logistic = jax.nn.sigmoid(values)
    return logistic * (1.0 + values * (1.0 - logistic))


def widen_cols(values):
    return jnp.pad(values, ((0, 0), (0, 0), (1, 1), (0, 0)))


def tap_columns(padded, frames, height, across):
    pieces = []
    for time_tap in range(3):
        for row_tap in range(3):
            for col_tap in range(3):
                start_time, start_row, start_col = (2 - time_tap, 2 - row_tap, 2 - col_tap)
                pieces.append(
                    padded[
                        start_time : start_time + frames,
                        start_row : start_row + height,
                        start_col : start_col + across,
                    ]
                )
    stacked = jnp.stack(pieces, 3)
    return stacked.reshape(frames * height * across, 27, padded.shape[3])


def backward_piece(columns, portion):
    return lax.dot_general(
        columns, portion, (((1, 2), (0, 2)), ((), ())), preferred_element_type=jnp.float32
    )


def kernel_grad(haloed, gradient, factor):
    height = gradient.shape[1]
    across = gradient.shape[2]
    channels = haloed.shape[3]
    split_grads = lax.all_to_all(gradient, "tm", split_axis=3, concat_axis=0, tiled=True)
    width_out = split_grads.shape[3]
    padded_grads = jnp.pad(split_grads, ((0, 2), (0, 0), (0, 0), (0, 0)))
    portion = lax.all_gather(haloed, "tm", axis=0, tiled=True)
    offset = jnp.int32(0)
    portion_frames = portion.shape[0]
    widened = widen_cols(portion)
    spatial = jnp.stack(
        [
            widened[:, row_tap : row_tap + height, col_tap : col_tap + across]
            for row_tap in range(3)
            for col_tap in range(3)
        ],
        3,
    )
    shifted_grads = jnp.stack(
        [
            lax.dynamic_slice_in_dim(padded_grads, offset + 2 - time_tap, portion_frames, 0)
            for time_tap in range(3)
        ],
        0,
    )
    contribution = lax.dot_general(
        spatial,
        shifted_grads,
        (((0, 1, 2), (1, 2, 3)), ((), ())),
        preferred_element_type=jnp.float32,
    )
    contribution = jnp.transpose(contribution, (2, 0, 1, 3)).reshape(27, channels, width_out)
    return lax.psum_scatter(contribution * factor, "rows", scatter_dimension=1, tiled=True)


def gathered_plan(inputs, cotangent, kernel):
    frames, height, across, channels = inputs.shape
    positions = frames * height * across
    rows_kernel = lax.all_gather(kernel, "rows", axis=1, tiled=True)
    act = jax.nn.silu(inputs.astype(jnp.float32)).astype(jnp.bfloat16)
    paired = jnp.concatenate([act, cotangent], 3)
    paired_rows = extended(paired, (("rows", 1),), 1)
    halo_act = paired_rows[:, :, :, :channels]
    halo_grad = paired_rows[:, :, :, channels:]
    split_bands = lax.all_to_all(halo_grad, "tm", split_axis=3, concat_axis=0, tiled=True)
    total_frames = split_bands.shape[0]
    padded_bands = jnp.pad(split_bands, ((0, 2), (0, 0), (0, 0), (0, 0)))
    cols_all = tap_columns(widen_cols(padded_bands), total_frames, height, across)
    partial_terms = backward_piece(cols_all, rows_kernel).reshape(
        total_frames // frames, positions, channels
    )
    grad_act = lax.psum_scatter(partial_terms, "tm", scatter_dimension=0, tiled=True)
    grad_act = grad_act.reshape(frames, height, across, channels)
    grad_inputs = (
        cotangent.astype(jnp.float32) + grad_act * silu_slope(inputs.astype(jnp.float32))
    ).astype(jnp.bfloat16)
    factor = float(frames * lax.axis_size("tm") * height * lax.axis_size("rows") * across) ** (-0.5)
    grad_kernel = kernel_grad(halo_act, cotangent, factor)
    return (grad_inputs, grad_kernel)


def exchange_fits(inputs, cotangent, kernel):
    frames, height, across, channels = inputs.shape
    groups, bands = lax.axis_size("tm"), lax.axis_size("rows")
    own_in, own_out = kernel.shape[1], kernel.shape[2]
    return (
        frames == 2
        and frames * height * across == LANES
        and across == 16
        and own_in == 16
        and own_out == LANES
        and groups == 2
        and bands == 16
        and channels == own_in * bands == own_out * groups
        and frames * groups * height * bands * across * own_out * 2 <= 4 * 2**20
    )


def exchange_kernel(
    groups, bands, factor,
    inputs_hbm, cot_hbm, kernel_hbm, grad_in_ref, grad_kernel_ref,
    inputs_ref, cot_ref, taps_ref, turned, grads, acts, act_edge, act_send, sums, part_send, part,
    back_send, back, spatial, share, share_in,
    load_sem, line_recv, side_recv, edge_recv, taps_recv, line_send, side_send, edge_send, taps_send,
    act_send_sem, act_recv_sem, act_edge_send, act_edge_recv, cross_send_sem, cross_recv_sem,
    part_send_sem, part_recv_sem, back_send_sem, back_recv_sem, share_send, share_recv,
):
    frames, height, across, channels = inputs_ref.shape
    own_in = grad_kernel_ref.shape[1]
    pair_in = 2 * own_in
    positions = frames * height * across
    chips = bands // 2
    depth = chips // 2
    near = bands // 2
    rows = height * near
    plane = rows * across
    all_frames = frames * groups
    half = LANES // 2

    group, band = lax.axis_index("tm"), lax.axis_index("rows")
    partner = (group + 1) % groups
    chip, core = band // 2, band % 2
    layer, column = chip // 2, chip % 2
    keeper = layer // 2
    at_home = keeper == core
    other_core = (group, chip * 2 + 1 - core)

    def device_of(layer_of, column_of, core_of):
        return (layer_of * 2 + column_of) * 2 + core_of

    def region(group_of, near_band):
        return grads.at[pl.ds(group_of * frames, frames), pl.ds(1 + near_band * height, height)]

    def wait_bytes(ref, sem):
        pltpu.make_async_copy(ref, ref, sem).wait()

    def remote(source, target, send_sem, recv_sem, device):
        return pltpu.make_async_remote_copy(
            src_ref=source, dst_ref=target, send_sem=send_sem, recv_sem=recv_sem,
            device_id=device, device_id_type=MESH,
        )

    load_inputs = pltpu.make_async_copy(inputs_hbm, inputs_ref, load_sem.at[0])
    load_cot = pltpu.make_async_copy(cot_hbm, cot_ref, load_sem.at[1])
    load_kernel = pltpu.make_async_copy(kernel_hbm, taps_ref.at[core], load_sem.at[2])
    load_inputs.start()
    load_cot.start()
    load_kernel.start()

    barrier = pltpu.get_barrier_semaphore()

    def greet(step, carry):
        pl.semaphore_signal(
            barrier, inc=1, device_id=(group, (band + step) % bands), device_id_type=MESH
        )
        return carry

    def greet_column(step, carry):
        pl.semaphore_signal(
            barrier, inc=1, device_id=(partner, device_of(step // 2, column, step % 2)),
            device_id_type=MESH,
        )
        return carry

    lax.fori_loop(1, bands, greet, 0)
    lax.fori_loop(0, 2 * depth, greet_column, 0)
    pl.semaphore_wait(barrier, bands - 1 + 2 * depth)

    own_part = cot_hbm.at[:, :, :, pl.ds(pl.multiple_of(group * LANES, LANES), LANES)]
    other_part = cot_hbm.at[:, :, :, pl.ds(pl.multiple_of(partner * LANES, LANES), LANES)]
    landing = region(group, band % near)

    def send_line(step, carry):
        turn = depth - 1 - step
        layer_of = (layer // 2 + turn // 2) % 2 * 2 + (layer + turn) % 2
        target = device_of(layer_of, column, keeper)
        arrival = line_recv.at[layer % 2, core]

        @pl.when(target == band)
        def _():
            pltpu.make_async_copy(own_part, landing, arrival.at[0]).start()

        @pl.when(target != band)
        def _():
            remote(own_part, landing, line_send, arrival.at[0], (group, target)).start()

        remote(other_part, landing, line_send, arrival.at[1], (partner, target)).start()
        return carry

    lax.fori_loop(0, depth, send_line, 0)
    load_kernel.wait()
    remote(taps_ref.at[core], taps_ref.at[core], taps_send, taps_recv, other_core).start()

    load_inputs.wait()
    values = inputs_ref[...].reshape(positions, channels).astype(jnp.float32)
    act = values * jax.nn.sigmoid(values)
    act_send[...] = act.T.astype(jnp.bfloat16).reshape(chips, pair_in, positions)

    def send_act(step, carry):
        to_chip = (chip + step) % chips
        target = to_chip * 2 + keeper
        source, place = act_send.at[to_chip], acts.at[group, band % near]

        @pl.when(target == band)
        def _():
            pltpu.make_async_copy(source, place, act_recv_sem).start()

        @pl.when(target != band)
        def _():
            remote(source, place, act_send_sem, act_recv_sem, (group, target)).start()

        return carry

    lax.fori_loop(0, chips, send_act, 0)

    lane = lax.broadcasted_iota(jnp.int32, (pair_in, plane), 1)
    col = lane % across
    low = lax.broadcasted_iota(jnp.int32, (pair_in, LANES), 1) < half

    def moved(block, by_col):
        if by_col == 0:
            return block
        cells = col[:, : block.shape[1]] + by_col
        block = pltpu.roll(block, (-by_col) % block.shape[1], 1)
        return jnp.where((cells >= 0) & (cells < across), block, 0.0)

    wait_bytes(taps_ref.at[1 - core], taps_recv)
    wide = 3 * own_in
    for time_tap in range(3):
        for row_tap in range(3):
            at = pl.ds(9 * time_tap + 3 * row_tap, 3)
            block = jnp.concatenate(
                [taps_ref[0, at].reshape(wide, LANES), taps_ref[1, at].reshape(wide, LANES)]
            ).astype(jnp.float32)
            block = jnp.concatenate([block, jnp.zeros((LANES - 2 * wide, LANES), jnp.float32)])
            turned[pl.ds(time_tap * LANES, LANES), pl.ds(row_tap * LANES, LANES)] = (
                block.T.astype(jnp.bfloat16)
            )
    spatial[pl.ds(0, 2)] = jnp.zeros((2,) + spatial.shape[1:], spatial.dtype)
    grads[:, pl.ds((rows + 1) * core, 1)] = jnp.zeros((all_frames, 1, across, LANES), jnp.bfloat16)

    def sum_rows(first, count):
        cells = [
            grads[frame, pl.ds(first, count)].reshape(count * across, LANES)
            for frame in range(all_frames)
        ] + [jnp.zeros((count * across, LANES), jnp.bfloat16)] * 2
        windows = jnp.concatenate(
            [
                jnp.concatenate([cells[frame + 2 - tap] for tap in range(3)], axis=1)
                for frame in range(all_frames)
            ],
            axis=0,
        )
        result = lax.dot_general(
            windows, turned[...], (((1,), (0,)), ((), ())), preferred_element_type=jnp.float32
        ).reshape(all_frames, count * across, 3 * LANES)
        start = first * across
        if not isinstance(start, int):
            start = pl.multiple_of(start, across)
        for row_tap in range(3):
            sums[row_tap, :, pl.ds(start, count * across)] = result[
                :, :, row_tap * LANES : (row_tap + 1) * LANES
            ]

    def all_of(near_band):
        return grads.at[:, pl.ds(1 + near_band * height, height)]

    edge_from = grads.at[:, pl.ds((1 - core) * rows + core, 1)]
    edge_to = grads.at[:, pl.ds(core * (rows + 1), 1)]
    edge_in = grads.at[:, pl.ds((1 - core) * (rows + 1), 1)]

    def pass_edge(near_band):
        @pl.when(near_band == (1 - core) * (near - 1))
        def _():
            remote(edge_from, edge_to, edge_send, edge_recv, other_core).start()

    def pass_line(turn, carry):
        odd = (layer + turn) % 2
        for core_of in range(2):
            near_band = odd * 4 + column * 2 + core_of
            for piece in range(groups):
                wait_bytes(region((group + piece) % groups, near_band),
                           line_recv.at[odd, core_of, piece])
            remote(
                all_of(near_band), all_of(near_band), side_send, side_recv.at[odd, core_of],
                (group, device_of(layer, 1 - column, core)),
            ).start()
            pass_edge(near_band)
        return carry

    def take_side(turn):
        odd = (layer + turn) % 2
        for core_of in range(2):
            near_band = odd * 4 + (1 - column) * 2 + core_of
            wait_bytes(all_of(near_band), side_recv.at[odd, core_of])
            pass_edge(near_band)

    lax.fori_loop(0, 2, pass_line, 0)

    wait_bytes(acts.at[group], act_recv_sem)
    remote(
        acts.at[group], acts.at[group], cross_send_sem, cross_recv_sem, (partner, band)
    ).start()

    def sum_chips(turn, carry):
        odd = (layer + turn) % 2
        far = turn // 2

        @pl.when(far == 1)
        def _():
            take_side(turn)

        sum_rows(1 + (odd * 2 + column + far - 2 * column * far) * 2 * height, 2 * height)
        return carry

    lax.fori_loop(0, 4, sum_chips, 0)

    wait_bytes(acts.at[partner], cross_recv_sem)
    remote(
        acts.at[:, (1 - core) * (near - 1)], act_edge, act_edge_send, act_edge_recv, other_core
    ).start()
    wait_bytes(edge_in, edge_recv)
    sum_rows(0, 1)
    sum_rows(rows + 1, 1)

    def grad_act_of(frame):
        mixed = None
        for row_tap in range(3):
            term = sums[row_tap, frame, pl.ds(across * (2 - row_tap), plane)]
            mixed = term if mixed is None else mixed + term
        mixed = mixed.T
        result = None
        for col_tap in range(3):
            at = col_tap * own_in
            term = jnp.concatenate([mixed[at : at + own_in], mixed[wide + at : wide + at + own_in]])
            term = moved(term, 1 - col_tap)
            result = term if result is None else result + term
        return result

    def shares(at, carry):
        owner = (partner + at // frames) % groups
        part_send[at] = grad_act_of(owner * frames + at % frames)

        @pl.when(at < frames)
        def _():
            remote(
                part_send.at[at], part.at[at], part_send_sem.at[at], part_recv_sem.at[at],
                (partner, band),
            ).start()

        return carry

    lax.fori_loop(0, all_frames, shares, 0)

    wait_bytes(act_edge, act_edge_recv)

    def shift_acts(group_of, carry):
        edge_tile = act_edge[group_of].astype(jnp.float32)
        above = jnp.where(core == 1, edge_tile, 0.0)
        below = jnp.where(core == 0, edge_tile, 0.0)
        for at in range(frames):
            tiles = []
            for pair in range(near // 2):
                x = acts[group_of, 2 * pair].astype(jnp.float32)
                y = acts[group_of, 2 * pair + 1].astype(jnp.float32)
                if at == 0:
                    tiles.append(jnp.where(low, x, pltpu.roll(y, half, 1)))
                else:
                    tiles.append(jnp.where(low, pltpu.roll(x, half, 1), y))
            whole = jnp.concatenate(tiles, axis=1)
            for col_tap in range(3):
                shifted = moved(whole, col_tap - 1)
                top = pltpu.roll(moved(above, col_tap - 1), (2 * LANES - at * half - 48) % LANES, 1)
                end = pltpu.roll(moved(below, col_tap - 1), (2 * LANES - at * half - across) % LANES, 1)
                repeat = plane // LANES
                top = jnp.concatenate([top] * repeat, axis=1)
                end = jnp.concatenate([end] * repeat, axis=1)
                up = jnp.where(lane < across, top, pltpu.roll(shifted, across, 1))
                down = jnp.where(lane >= plane - across, end, pltpu.roll(shifted, plane - across, 1))
                for row_tap, block in enumerate((up, shifted, down)):
                    tap = 3 * row_tap + col_tap
                    spatial[2 + group_of * frames + at, pl.ds(tap * pair_in, pair_in)] = (
                        block.astype(jnp.bfloat16)
                    )
        return carry

    lax.fori_loop(0, groups, shift_acts, 0)
    share[...] = jnp.zeros_like(share)

    def kernel_taps(frame, carry):
        cells = grads[frame, pl.ds(1, rows)].reshape(plane, LANES)
        for time_tap in range(3):
            term = lax.dot_general(
                spatial[frame + time_tap], cells, (((1,), (0,)), ((), ())),
                preferred_element_type=jnp.float32,
            ).reshape(9, 2, own_in, LANES)
            own = pl.ds(9 * time_tap, 9)
            for core_of in range(2):
                share[core_of, own] = share[core_of, own] + term[:, core_of]
        return carry

    lax.fori_loop(0, frames, kernel_taps, 0)
    for at in range(frames):
        wait_bytes(part.at[at], part_recv_sem.at[at])
    first, second = [part_send[frames + at] + part[at] for at in range(frames)]
    for pair in range(near // 2):
        x = first[:, pair * LANES : (pair + 1) * LANES]
        y = second[:, pair * LANES : (pair + 1) * LANES]
        back_send[2 * pair] = jnp.where(low, x, pltpu.roll(y, half, 1))
        back_send[2 * pair + 1] = jnp.where(low, pltpu.roll(x, half, 1), y)

    def send_back(step, carry):
        near_band = (band + step) % near
        target = core * near + near_band
        source, place = back_send.at[near_band], back.at[chip]

        @pl.when(target == band)
        def _():
            pltpu.make_async_copy(source, place, back_recv_sem).start()

        @pl.when(target != band)
        def _():
            remote(source, place, back_send_sem, back_recv_sem, (group, target)).start()

        return carry

    lax.fori_loop(0, near, send_back, 0)

    lax.fori_loop(frames, all_frames, kernel_taps, 0)
    remote(share.at[1 - core], share_in, share_send, share_recv, other_core).start()

    wait_bytes(back, back_recv_sem)
    grad_act = back[...].reshape(channels, positions).T
    values = inputs_ref[...].reshape(positions, channels).astype(jnp.float32)
    load_cot.wait()
    cot = cot_ref[...].reshape(positions, channels).astype(jnp.float32)
    grad_in = cot + grad_act * silu_slope(values)
    grad_in_ref[...] = grad_in.astype(jnp.bfloat16).reshape(grad_in_ref.shape)
    wait_bytes(share_in, share_recv)
    grad_kernel_ref[...] = (share[core] + share_in[...]) * factor

    sent = 2 * depth

    @pl.when(at_home)
    def _():
        wait_bytes(grads.at[pl.ds(0, frames), pl.ds(0, height * (sent - 1))], line_send)
        wait_bytes(acts.at[0, pl.ds(0, chips - 1)], act_send_sem)
        wait_bytes(back.at[pl.ds(0, near - 1)], back_send_sem)

    @pl.when(jnp.logical_not(at_home))
    def _():
        wait_bytes(grads.at[pl.ds(0, frames), pl.ds(0, height * sent)], line_send)
        wait_bytes(acts.at[0, pl.ds(0, chips)], act_send_sem)
        wait_bytes(back.at[pl.ds(0, near)], back_send_sem)

    wait_bytes(grads.at[:, pl.ds(0, 4 * height)], side_send)
    wait_bytes(edge_from, edge_send)
    wait_bytes(taps_ref.at[core], taps_send)
    wait_bytes(act_edge, act_edge_send)
    wait_bytes(acts.at[group], cross_send_sem)
    for at in range(frames):
        wait_bytes(part_send.at[at], part_send_sem.at[at])
    wait_bytes(share_in, share_send)


def exchange_plan(inputs, cotangent, kernel):
    frames, height, across, channels = inputs.shape
    taps, own_in, own_out = kernel.shape
    groups, bands = lax.axis_size("tm"), lax.axis_size("rows")
    positions = frames * height * across
    all_frames, chips, near = frames * groups, bands // 2, bands // 2
    rows = height * near
    plane = rows * across
    factor = float(all_frames * 2 * plane) ** (-0.5)
    dma = pltpu.SemaphoreType.DMA
    bf16, f32 = jnp.bfloat16, jnp.float32
    return pl.pallas_call(
        functools.partial(exchange_kernel, groups, bands, factor),
        out_shape=(pltpu.VMEM(inputs.shape, bf16), pltpu.VMEM(kernel.shape, f32)),
        in_specs=[pl.BlockSpec(memory_space=pltpu.HBM)] * 3,
        out_specs=[pl.BlockSpec(memory_space=pltpu.VMEM)] * 2,
        scratch_shapes=[
            pltpu.VMEM(inputs.shape, bf16),
            pltpu.VMEM(cotangent.shape, bf16),
            pltpu.VMEM((2,) + kernel.shape, bf16),
            pltpu.VMEM((3 * LANES, 3 * LANES), bf16),
            pltpu.VMEM((all_frames, rows + 2, across, own_out), bf16),
            pltpu.VMEM((groups, near, 2 * own_in, positions), bf16),
            pltpu.VMEM((groups, 2 * own_in, positions), bf16),
            pltpu.VMEM((chips, 2 * own_in, positions), bf16),
            pltpu.VMEM((3, all_frames, plane + 2 * across, LANES), f32),
            pltpu.VMEM((all_frames, 2 * own_in, plane), f32),
            pltpu.VMEM((frames, 2 * own_in, plane), f32),
            pltpu.VMEM((near, 2 * own_in, positions), f32),
            pltpu.VMEM((chips, 2 * own_in, positions), f32),
            pltpu.VMEM((all_frames + 2, 18 * own_in, plane), bf16),
            pltpu.VMEM((2,) + kernel.shape, f32),
            pltpu.VMEM(kernel.shape, f32),
            dma((3,)),
            dma((2, 2, groups)),
            dma((2, 2)),
        ] + [dma] * 12 + [dma((frames,))] * 2 + [dma] * 4,
        compiler_params=pltpu.CompilerParams(
            collective_id=0, has_side_effects=True, vmem_limit_bytes=60 * 2**20
        ),
    )(inputs, cotangent, kernel)


def local(inputs, cotangent, kernel):
    if exchange_fits(inputs, cotangent, kernel):
        return exchange_plan(inputs, cotangent, kernel)
    return gathered_plan(inputs, cotangent, kernel)


def solution(mesh):
    return jax.shard_map(
        local,
        mesh=mesh,
        in_specs=(P("tm", "rows", None, None), P("tm", "rows", None, None), P(None, "rows", "tm")),
        out_specs=(P("tm", "rows", None, None), P(None, "rows", "tm")),
        check_vma=False,
    )
```

```python
import functools

import jax
import jax.numpy as jnp
from jax import lax
from jax.experimental import pallas as pl
from jax.experimental.pallas import tpu as pltpu
from jax.sharding import PartitionSpec as P

MESH = pl.DeviceIdType.MESH
LANES = 128


def extended(block, sides, width):
    for axis, dim in sides:
        count = lax.axis_size(axis)
        forward = [(i, i + 1) for i in range(count - 1)]
        backward = [(target, source) for source, target in forward]
        low = lax.ppermute(
            lax.slice_in_dim(block, block.shape[dim] - width, None, axis=dim), axis, forward
        )
        high = lax.ppermute(lax.slice_in_dim(block, 0, width, axis=dim), axis, backward)
        block = jnp.concatenate([low, block, high], axis=dim)
    return block


def silu_slope(values):
    logistic = jax.nn.sigmoid(values)
    return logistic * (1.0 + values * (1.0 - logistic))


def widen_cols(values):
    return jnp.pad(values, ((0, 0), (0, 0), (1, 1), (0, 0)))


def tap_columns(padded, frames, height, across):
    pieces = []
    for time_tap in range(3):
        for row_tap in range(3):
            for col_tap in range(3):
                start_time, start_row, start_col = (2 - time_tap, 2 - row_tap, 2 - col_tap)
                pieces.append(
                    padded[
                        start_time : start_time + frames,
                        start_row : start_row + height,
                        start_col : start_col + across,
                    ]
                )
    stacked = jnp.stack(pieces, 3)
    return stacked.reshape(frames * height * across, 27, padded.shape[3])


def backward_piece(columns, portion):
    return lax.dot_general(
        columns, portion, (((1, 2), (0, 2)), ((), ())), preferred_element_type=jnp.float32
    )


def kernel_grad(haloed, gradient, factor):
    height = gradient.shape[1]
    across = gradient.shape[2]
    channels = haloed.shape[3]
    split_grads = lax.all_to_all(gradient, "tm", split_axis=3, concat_axis=0, tiled=True)
    width_out = split_grads.shape[3]
    padded_grads = jnp.pad(split_grads, ((0, 2), (0, 0), (0, 0), (0, 0)))
    portion = lax.all_gather(haloed, "tm", axis=0, tiled=True)
    offset = jnp.int32(0)
    portion_frames = portion.shape[0]
    widened = widen_cols(portion)
    spatial = jnp.stack(
        [
            widened[:, row_tap : row_tap + height, col_tap : col_tap + across]
            for row_tap in range(3)
            for col_tap in range(3)
        ],
        3,
    )
    shifted_grads = jnp.stack(
        [
            lax.dynamic_slice_in_dim(padded_grads, offset + 2 - time_tap, portion_frames, 0)
            for time_tap in range(3)
        ],
        0,
    )
    contribution = lax.dot_general(
        spatial,
        shifted_grads,
        (((0, 1, 2), (1, 2, 3)), ((), ())),
        preferred_element_type=jnp.float32,
    )
    contribution = jnp.transpose(contribution, (2, 0, 1, 3)).reshape(27, channels, width_out)
    return lax.psum_scatter(contribution * factor, "rows", scatter_dimension=1, tiled=True)


def gathered_plan(inputs, cotangent, kernel):
    frames, height, across, channels = inputs.shape
    positions = frames * height * across
    rows_kernel = lax.all_gather(kernel, "rows", axis=1, tiled=True)
    act = jax.nn.silu(inputs.astype(jnp.float32)).astype(jnp.bfloat16)
    paired = jnp.concatenate([act, cotangent], 3)
    paired_rows = extended(paired, (("rows", 1),), 1)
    halo_act = paired_rows[:, :, :, :channels]
    halo_grad = paired_rows[:, :, :, channels:]
    split_bands = lax.all_to_all(halo_grad, "tm", split_axis=3, concat_axis=0, tiled=True)
    total_frames = split_bands.shape[0]
    padded_bands = jnp.pad(split_bands, ((0, 2), (0, 0), (0, 0), (0, 0)))
    cols_all = tap_columns(widen_cols(padded_bands), total_frames, height, across)
    partial_terms = backward_piece(cols_all, rows_kernel).reshape(
        total_frames // frames, positions, channels
    )
    grad_act = lax.psum_scatter(partial_terms, "tm", scatter_dimension=0, tiled=True)
    grad_act = grad_act.reshape(frames, height, across, channels)
    grad_inputs = (
        cotangent.astype(jnp.float32) + grad_act * silu_slope(inputs.astype(jnp.float32))
    ).astype(jnp.bfloat16)
    factor = float(frames * lax.axis_size("tm") * height * lax.axis_size("rows") * across) ** (-0.5)
    grad_kernel = kernel_grad(halo_act, cotangent, factor)
    return (grad_inputs, grad_kernel)


def exchange_fits(inputs, cotangent, kernel):
    frames, height, across, channels = inputs.shape
    groups, bands = lax.axis_size("tm"), lax.axis_size("rows")
    own_in, own_out = kernel.shape[1], kernel.shape[2]
    return (
        frames == 2
        and frames * height * across == LANES
        and across == 16
        and own_in == 16
        and own_out == LANES
        and groups == 2
        and bands == 16
        and channels == own_in * bands == own_out * groups
        and frames * groups * height * bands * across * own_out * 2 <= 4 * 2**20
    )


def exchange_kernel(
    groups, bands, factor,
    inputs_hbm, cot_hbm, kernel_hbm, grad_in_ref, grad_kernel_ref,
    inputs_ref, cot_ref, taps_ref, turned, grads, acts, act_edge, act_send, sums, part_send, part,
    back_send, back, spatial, share, share_in,
    load_sem, line_recv, side_recv, edge_recv, taps_recv, line_send, side_send, edge_send, taps_send,
    act_send_sem, act_recv_sem, act_edge_send, act_edge_recv, cross_send_sem, cross_recv_sem,
    part_send_sem, part_recv_sem, back_send_sem, back_recv_sem, share_send, share_recv,
):
    frames, height, across, channels = inputs_ref.shape
    own_in = grad_kernel_ref.shape[1]
    pair_in = 2 * own_in
    positions = frames * height * across
    chips = bands // 2
    depth = chips // 2
    near = bands // 2
    rows = height * near
    plane = rows * across
    all_frames = frames * groups
    half = LANES // 2

    group, band = lax.axis_index("tm"), lax.axis_index("rows")
    partner = (group + 1) % groups
    chip, core = band // 2, band % 2
    layer, column = chip // 2, chip % 2
    keeper = layer // 2
    at_home = keeper == core
    other_core = (group, chip * 2 + 1 - core)

    def device_of(layer_of, column_of, core_of):
        return (layer_of * 2 + column_of) * 2 + core_of

    def region(group_of, near_band):
        return grads.at[pl.ds(group_of * frames, frames), pl.ds(1 + near_band * height, height)]

    def wait_bytes(ref, sem):
        pltpu.make_async_copy(ref, ref, sem).wait()

    def remote(source, target, send_sem, recv_sem, device):
        return pltpu.make_async_remote_copy(
            src_ref=source, dst_ref=target, send_sem=send_sem, recv_sem=recv_sem,
            device_id=device, device_id_type=MESH,
        )

    load_inputs = pltpu.make_async_copy(inputs_hbm, inputs_ref, load_sem.at[0])
    load_cot = pltpu.make_async_copy(cot_hbm, cot_ref, load_sem.at[1])
    load_kernel = pltpu.make_async_copy(kernel_hbm, taps_ref.at[core], load_sem.at[2])
    load_inputs.start()
    load_cot.start()
    load_kernel.start()

    barrier = pltpu.get_barrier_semaphore()

    def greet(step, carry):
        pl.semaphore_signal(
            barrier, inc=1, device_id=(group, (band + step) % bands), device_id_type=MESH
        )
        return carry

    def greet_column(step, carry):
        pl.semaphore_signal(
            barrier, inc=1, device_id=(partner, device_of(step // 2, column, step % 2)),
            device_id_type=MESH,
        )
        return carry

    lax.fori_loop(1, bands, greet, 0)
    lax.fori_loop(0, 2 * depth, greet_column, 0)
    pl.semaphore_wait(barrier, bands - 1 + 2 * depth)

    own_part = cot_hbm.at[:, :, :, pl.ds(pl.multiple_of(group * LANES, LANES), LANES)]
    other_part = cot_hbm.at[:, :, :, pl.ds(pl.multiple_of(partner * LANES, LANES), LANES)]
    landing = region(group, band % near)

    def send_line(step, carry):
        turn = depth - 1 - step
        layer_of = (layer // 2 + turn // 2) % 2 * 2 + (layer + turn) % 2
        target = device_of(layer_of, column, keeper)
        arrival = line_recv.at[layer % 2, core]

        @pl.when(target == band)
        def _():
            pltpu.make_async_copy(own_part, landing, arrival.at[0]).start()

        @pl.when(target != band)
        def _():
            remote(own_part, landing, line_send, arrival.at[0], (group, target)).start()

        remote(other_part, landing, line_send, arrival.at[1], (partner, target)).start()
        return carry

    lax.fori_loop(0, depth, send_line, 0)
    load_kernel.wait()
    remote(taps_ref.at[core], taps_ref.at[core], taps_send, taps_recv, other_core).start()

    load_inputs.wait()
    values = inputs_ref[...].reshape(positions, channels).astype(jnp.float32)
    act = values * jax.nn.sigmoid(values)
    act_send[...] = act.T.astype(jnp.bfloat16).reshape(chips, pair_in, positions)

    def send_act(step, carry):
        to_chip = (chip + step) % chips
        target = to_chip * 2 + keeper
        source, place = act_send.at[to_chip], acts.at[group, band % near]

        @pl.when(target == band)
        def _():
            pltpu.make_async_copy(source, place, act_recv_sem).start()

        @pl.when(target != band)
        def _():
            remote(source, place, act_send_sem, act_recv_sem, (group, target)).start()

        return carry

    lax.fori_loop(0, chips, send_act, 0)

    lane = lax.broadcasted_iota(jnp.int32, (pair_in, plane), 1)
    col = lane % across
    low = lax.broadcasted_iota(jnp.int32, (pair_in, LANES), 1) < half

    def moved(block, by_col):
        if by_col == 0:
            return block
        cells = col[:, : block.shape[1]] + by_col
        block = pltpu.roll(block, (-by_col) % block.shape[1], 1)
        return jnp.where((cells >= 0) & (cells < across), block, 0.0)

    wait_bytes(taps_ref.at[1 - core], taps_recv)
    wide = 3 * own_in
    for time_tap in range(3):
        for row_tap in range(3):
            at = pl.ds(9 * time_tap + 3 * row_tap, 3)
            block = jnp.concatenate(
                [taps_ref[0, at].reshape(wide, LANES), taps_ref[1, at].reshape(wide, LANES)]
            ).astype(jnp.float32)
            block = jnp.concatenate([block, jnp.zeros((LANES - 2 * wide, LANES), jnp.float32)])
            turned[pl.ds(time_tap * LANES, LANES), pl.ds(row_tap * LANES, LANES)] = (
                block.T.astype(jnp.bfloat16)
            )
    spatial[pl.ds(0, 2)] = jnp.zeros((2,) + spatial.shape[1:], spatial.dtype)
    grads[:, pl.ds((rows + 1) * core, 1)] = jnp.zeros((all_frames, 1, across, LANES), jnp.bfloat16)

    def sum_rows(first, count):
        cells = [
            grads[frame, pl.ds(first, count)].reshape(count * across, LANES)
            for frame in range(all_frames)
        ] + [jnp.zeros((count * across, LANES), jnp.bfloat16)] * 2
        windows = jnp.concatenate(
            [
                jnp.concatenate([cells[frame + 2 - tap] for tap in range(3)], axis=1)
                for frame in range(all_frames)
            ],
            axis=0,
        )
        result = lax.dot_general(
            windows, turned[...], (((1,), (0,)), ((), ())), preferred_element_type=jnp.float32
        ).reshape(all_frames, count * across, 3 * LANES)
        start = first * across
        if not isinstance(start, int):
            start = pl.multiple_of(start, across)
        for row_tap in range(3):
            sums[row_tap, :, pl.ds(start, count * across)] = result[
                :, :, row_tap * LANES : (row_tap + 1) * LANES
            ]

    def all_of(near_band):
        return grads.at[:, pl.ds(1 + near_band * height, height)]

    edge_from = grads.at[:, pl.ds((1 - core) * rows + core, 1)]
    edge_to = grads.at[:, pl.ds(core * (rows + 1), 1)]
    edge_in = grads.at[:, pl.ds((1 - core) * (rows + 1), 1)]

    def pass_edge(near_band):
        @pl.when(near_band == (1 - core) * (near - 1))
        def _():
            remote(edge_from, edge_to, edge_send, edge_recv, other_core).start()

    def pass_line(turn, carry):
        odd = (layer + turn) % 2
        for core_of in range(2):
            near_band = odd * 4 + column * 2 + core_of
            for piece in range(groups):
                wait_bytes(region((group + piece) % groups, near_band),
                           line_recv.at[odd, core_of, piece])
            remote(
                all_of(near_band), all_of(near_band), side_send, side_recv.at[odd, core_of],
                (group, device_of(layer, 1 - column, core)),
            ).start()
            pass_edge(near_band)
        return carry

    def take_side(turn):
        odd = (layer + turn) % 2
        for core_of in range(2):
            near_band = odd * 4 + (1 - column) * 2 + core_of
            wait_bytes(all_of(near_band), side_recv.at[odd, core_of])
            pass_edge(near_band)

    lax.fori_loop(0, 2, pass_line, 0)

    wait_bytes(acts.at[group], act_recv_sem)
    remote(
        acts.at[group], acts.at[group], cross_send_sem, cross_recv_sem, (partner, band)
    ).start()

    def sum_chips(turn, carry):
        odd = (layer + turn) % 2
        far = turn // 2

        @pl.when(far == 1)
        def _():
            take_side(turn)

        sum_rows(1 + (odd * 2 + column + far - 2 * column * far) * 2 * height, 2 * height)
        return carry

    lax.fori_loop(0, 4, sum_chips, 0)

    wait_bytes(acts.at[partner], cross_recv_sem)
    remote(
        acts.at[:, (1 - core) * (near - 1)], act_edge, act_edge_send, act_edge_recv, other_core
    ).start()
    wait_bytes(edge_in, edge_recv)
    sum_rows(0, 1)
    sum_rows(rows + 1, 1)

    def grad_act_of(frame):
        mixed = None
        for row_tap in range(3):
            term = sums[row_tap, frame, pl.ds(across * (2 - row_tap), plane)]
            mixed = term if mixed is None else mixed + term
        mixed = mixed.T
        result = None
        for col_tap in range(3):
            at = col_tap * own_in
            term = jnp.concatenate([mixed[at : at + own_in], mixed[wide + at : wide + at + own_in]])
            term = moved(term, 1 - col_tap)
            result = term if result is None else result + term
        return result

    def shares(at, carry):
        owner = (partner + at // frames) % groups
        part_send[at] = grad_act_of(owner * frames + at % frames)

        @pl.when(at < frames)
        def _():
            remote(
                part_send.at[at], part.at[at], part_send_sem.at[at], part_recv_sem.at[at],
                (partner, band),
            ).start()

        return carry

    lax.fori_loop(0, all_frames, shares, 0)

    wait_bytes(act_edge, act_edge_recv)

    def shift_acts(group_of, carry):
        edge_tile = act_edge[group_of].astype(jnp.float32)
        above = jnp.where(core == 1, edge_tile, 0.0)
        below = jnp.where(core == 0, edge_tile, 0.0)
        for at in range(frames):
            tiles = []
            for pair in range(near // 2):
                x = acts[group_of, 2 * pair].astype(jnp.float32)
                y = acts[group_of, 2 * pair + 1].astype(jnp.float32)
                if at == 0:
                    tiles.append(jnp.where(low, x, pltpu.roll(y, half, 1)))
                else:
                    tiles.append(jnp.where(low, pltpu.roll(x, half, 1), y))
            whole = jnp.concatenate(tiles, axis=1)
            for col_tap in range(3):
                shifted = moved(whole, col_tap - 1)
                top = pltpu.roll(moved(above, col_tap - 1), (2 * LANES - at * half - 48) % LANES, 1)
                end = pltpu.roll(moved(below, col_tap - 1), (2 * LANES - at * half - across) % LANES, 1)
                repeat = plane // LANES
                top = jnp.concatenate([top] * repeat, axis=1)
                end = jnp.concatenate([end] * repeat, axis=1)
                up = jnp.where(lane < across, top, pltpu.roll(shifted, across, 1))
                down = jnp.where(lane >= plane - across, end, pltpu.roll(shifted, plane - across, 1))
                for row_tap, block in enumerate((up, shifted, down)):
                    tap = 3 * row_tap + col_tap
                    spatial[2 + group_of * frames + at, pl.ds(tap * pair_in, pair_in)] = (
                        block.astype(jnp.bfloat16)
                    )
        return carry

    lax.fori_loop(0, groups, shift_acts, 0)
    share[...] = jnp.zeros_like(share)

    for at in range(frames):
        wait_bytes(part.at[at], part_recv_sem.at[at])
    first, second = [part_send[frames + at] + part[at] for at in range(frames)]
    for pair in range(near // 2):
        x = first[:, pair * LANES : (pair + 1) * LANES]
        y = second[:, pair * LANES : (pair + 1) * LANES]
        back_send[2 * pair] = jnp.where(low, x, pltpu.roll(y, half, 1))
        back_send[2 * pair + 1] = jnp.where(low, pltpu.roll(x, half, 1), y)

    def send_back(step, carry):
        near_band = (band + step) % near
        target = core * near + near_band
        source, place = back_send.at[near_band], back.at[chip]

        @pl.when(target == band)
        def _():
            pltpu.make_async_copy(source, place, back_recv_sem).start()

        @pl.when(target != band)
        def _():
            remote(source, place, back_send_sem, back_recv_sem, (group, target)).start()

        return carry

    lax.fori_loop(0, near, send_back, 0)

    def kernel_taps(frame, carry):
        cells = grads[frame, pl.ds(1, rows)].reshape(plane, LANES)
        for time_tap in range(3):
            term = lax.dot_general(
                spatial[frame + time_tap], cells, (((1,), (0,)), ((), ())),
                preferred_element_type=jnp.float32,
            ).reshape(9, 2, own_in, LANES)
            own = pl.ds(9 * time_tap, 9)
            for core_of in range(2):
                share[core_of, own] = share[core_of, own] + term[:, core_of]
        return carry

    lax.fori_loop(0, all_frames, kernel_taps, 0)
    remote(share.at[1 - core], share_in, share_send, share_recv, other_core).start()

    wait_bytes(back, back_recv_sem)
    grad_act = back[...].reshape(channels, positions).T
    values = inputs_ref[...].reshape(positions, channels).astype(jnp.float32)
    load_cot.wait()
    cot = cot_ref[...].reshape(positions, channels).astype(jnp.float32)
    grad_in = cot + grad_act * silu_slope(values)
    grad_in_ref[...] = grad_in.astype(jnp.bfloat16).reshape(grad_in_ref.shape)
    wait_bytes(share_in, share_recv)
    grad_kernel_ref[...] = (share[core] + share_in[...]) * factor

    sent = 2 * depth

    @pl.when(at_home)
    def _():
        wait_bytes(grads.at[pl.ds(0, frames), pl.ds(0, height * (sent - 1))], line_send)
        wait_bytes(acts.at[0, pl.ds(0, chips - 1)], act_send_sem)
        wait_bytes(back.at[pl.ds(0, near - 1)], back_send_sem)

    @pl.when(jnp.logical_not(at_home))
    def _():
        wait_bytes(grads.at[pl.ds(0, frames), pl.ds(0, height * sent)], line_send)
        wait_bytes(acts.at[0, pl.ds(0, chips)], act_send_sem)
        wait_bytes(back.at[pl.ds(0, near)], back_send_sem)

    wait_bytes(grads.at[:, pl.ds(0, 4 * height)], side_send)
    wait_bytes(edge_from, edge_send)
    wait_bytes(taps_ref.at[core], taps_send)
    wait_bytes(act_edge, act_edge_send)
    wait_bytes(acts.at[group], cross_send_sem)
    for at in range(frames):
        wait_bytes(part_send.at[at], part_send_sem.at[at])
    wait_bytes(share_in, share_send)


def exchange_plan(inputs, cotangent, kernel):
    frames, height, across, channels = inputs.shape
    taps, own_in, own_out = kernel.shape
    groups, bands = lax.axis_size("tm"), lax.axis_size("rows")
    positions = frames * height * across
    all_frames, chips, near = frames * groups, bands // 2, bands // 2
    rows = height * near
    plane = rows * across
    factor = float(all_frames * 2 * plane) ** (-0.5)
    dma = pltpu.SemaphoreType.DMA
    bf16, f32 = jnp.bfloat16, jnp.float32
    return pl.pallas_call(
        functools.partial(exchange_kernel, groups, bands, factor),
        out_shape=(pltpu.VMEM(inputs.shape, bf16), pltpu.VMEM(kernel.shape, f32)),
        in_specs=[pl.BlockSpec(memory_space=pltpu.HBM)] * 3,
        out_specs=[pl.BlockSpec(memory_space=pltpu.VMEM)] * 2,
        scratch_shapes=[
            pltpu.VMEM(inputs.shape, bf16),
            pltpu.VMEM(cotangent.shape, bf16),
            pltpu.VMEM((2,) + kernel.shape, bf16),
            pltpu.VMEM((3 * LANES, 3 * LANES), bf16),
            pltpu.VMEM((all_frames, rows + 2, across, own_out), bf16),
            pltpu.VMEM((groups, near, 2 * own_in, positions), bf16),
            pltpu.VMEM((groups, 2 * own_in, positions), bf16),
            pltpu.VMEM((chips, 2 * own_in, positions), bf16),
            pltpu.VMEM((3, all_frames, plane + 2 * across, LANES), f32),
            pltpu.VMEM((all_frames, 2 * own_in, plane), f32),
            pltpu.VMEM((frames, 2 * own_in, plane), f32),
            pltpu.VMEM((near, 2 * own_in, positions), f32),
            pltpu.VMEM((chips, 2 * own_in, positions), f32),
            pltpu.VMEM((all_frames + 2, 18 * own_in, plane), bf16),
            pltpu.VMEM((2,) + kernel.shape, f32),
            pltpu.VMEM(kernel.shape, f32),
            dma((3,)),
            dma((2, 2, groups)),
            dma((2, 2)),
        ] + [dma] * 12 + [dma((frames,))] * 2 + [dma] * 4,
        compiler_params=pltpu.CompilerParams(
            collective_id=0, has_side_effects=True, vmem_limit_bytes=60 * 2**20
        ),
    )(inputs, cotangent, kernel)


def local(inputs, cotangent, kernel):
    if exchange_fits(inputs, cotangent, kernel):
        return exchange_plan(inputs, cotangent, kernel)
    return gathered_plan(inputs, cotangent, kernel)


def solution(mesh):
    return jax.shard_map(
        local,
        mesh=mesh,
        in_specs=(P("tm", "rows", None, None), P("tm", "rows", None, None), P(None, "rows", "tm")),
        out_specs=(P("tm", "rows", None, None), P(None, "rows", "tm")),
        check_vma=False,
    )
```
